32 devices in a mesh: blk: 8 (over z, x), tm: 4 (over y, core).
Axes of the slice: x: 2, y: 2, z: 4, core: 2. Of those that a mesh axis runs over, the one named last changes fastest.
Arguments:
- density: bfloat16 [768, 256, 128], P('blk', 'tm'), may hold values from 0.5 to 2
- flow_rest: bfloat16 [768, 4, 256, 128], P('blk', None, 'tm'), may hold values from -6 to 6
- dest: int32 [768, 1], P('blk'), may hold values from 0 to 7; in each aligned block of 96 rows (0 to 95, 96 to 191, ...) at most 24 rows name the same one
- weights: bfloat16 [8, 64, 256, 128], P('blk', None, 'tm'), may hold values from -0.0024414062 to 0.0024414062
- directions: float32 [64, 3], replicated, may hold values from -4 to 4
- bins: int32 [64, 8], P(None, 'blk'), may hold values from 0 to 255
Outputs:
- record: float32 [64, 256], P('blk', 'tm')
The draws below stay inside these ranges and needn't reach their ends.
Inputs may be any that keep to these rules, and one draw needn't show every extreme that they name: `dest`: each row names one source block; the rows of one partition name any block at most 24 times, and some partition names some block exactly 24 times.
All inputs are finite; a program needn't handle non-finite values.
Results may differ from the reference program's by a relative error of at most 0.0003.
Values may be sent and summed in bfloat16 or wider, within the bound.
No kernel may reach another device: no remote copies, remote signals or barrier semaphores. Data moves between devices by JAX's collectives and lax.ppermute only.
A program may use at most 128 MiB of HBM per device.

```python
import math
import jax
import jax.numpy as jnp
import numpy as np
from jax import lax

W = 128
NT = 256
NOBS = 64
R_DEV = 96
CAP = 24
ROWS = 768
N_BLK = 8


def place_ends(result, own_key, low, largest):
    longest = result.shape.index(max(result.shape))
    spots = []
    for shift in (0, 1):
        where = [jax.random.randint(jax.random.fold_in(own_key, axis), (), 0, length) for axis, length in enumerate(result.shape)]
        where[longest] = (where[longest] + shift) % result.shape[longest]
        spots.append(tuple(where))
    return result.at[spots[0]].set(low).at[spots[1]].set(largest)


def raised(drawn, stream_key, source, target, parts, factor):
    owner, partner = [(jnp.arange(drawn.shape[axis_at]) // (drawn.shape[axis_at] // parts)).reshape([-1 if axis == axis_at else 1 for axis in range(drawn.ndim)]) for axis_at in (source, target)]
    chosen = jax.random.permutation(stream_key, parts)[partner]
    strong = (owner == chosen) | (owner == (partner + parts // 2) % parts)
    return jnp.where(strong, factor * drawn, drawn)


def block_levels(rng, shape, split, low, high):
    def one(position, blocks):
        steps = jax.random.uniform(jax.random.fold_in(jax.random.fold_in(rng, 6), position), (blocks,), jnp.float32, low / len(split), high / len(split))
        return jnp.repeat(jnp.exp(steps), shape[position] // blocks).reshape((-1,) + (1,) * (len(shape) - position - 1))

    level = one(*split[0])
    for cut in split[1:]:
        level = level * one(*cut)
    return level


def routed_block(rng, own, number, rows, amount, top, reach, lean):
    sequence = jax.random.permutation(rng, amount)
    packed, usual = load_shares(amount, rows * top, reach, lean, True), load_shares(amount, rows * top, reach, lean, False)
    places = jnp.arange(amount)

    def named(tallies, turn):
        used = int((tallies > 0).sum())
        fixed = max(1, used // 4)
        passed = fixed + (places - fixed + turn * (used - fixed)) % max(1, amount - fixed)
        return jnp.zeros((amount,), jnp.int32).at[sequence[jnp.where(places < fixed, places, passed)]].set(jnp.asarray(tallies, jnp.int32))

    tallies = jnp.where(number % 4 == 0, named(packed, number // 4), named(usual, number - number // 4 - 1))
    mixed = jax.random.permutation(jax.random.fold_in(own, 3), amount)
    source_of, receiver = mixed[0:amount // 2 * 2:2], mixed[1:amount // 2 * 2:2]
    room = jnp.minimum(tallies[source_of] - 1, reach - tallies[receiver]) // 2
    room = jnp.where((source_of == sequence[0]) | (receiver == sequence[0]) | (tallies[receiver] == 0), 0, jnp.maximum(room, 0))
    passed = jax.random.randint(jax.random.fold_in(own, 4), (amount // 2,), 0, 1 << 20) % (room + 1)
    tallies = tallies.at[source_of].add(-passed).at[receiver].add(passed)
    items = jnp.searchsorted(jnp.cumsum(tallies), jnp.arange(rows * top), side="right").astype(jnp.int32)
    listing = items.reshape(top, rows).T
    listing = listing[jax.random.permutation(jax.random.fold_in(own, 1), rows)]
    turn = jax.random.randint(jax.random.fold_in(own, 2), (rows, 1), 0, top)
    return jnp.take_along_axis(listing, (jnp.arange(top)[None, :] + turn) % top, axis=1)


def load_shares(amount, total, reach, lean, full):
    loads = [(1 << 20) // math.isqrt(standing ** lean) + 1 for standing in range(1, amount + 1)]
    largest = reach if full else min(reach, max(-(-total // amount), total * loads[0] // sum(loads)))
    least = 1 if total - largest >= amount - 1 else 0
    counts, spare = [largest] + [least] * (amount - 1), total - largest - least * (amount - 1)
    while spare > 0:
        candidates = [i for i in range(1, amount) if counts[i] < largest] or [i for i in range(1, amount) if counts[i] < reach]
        whole, remaining = sum([loads[i] for i in candidates]), spare
        for i in candidates:
            addition = min(reach - counts[i], max(1, remaining * loads[i] // whole), spare)
            counts[i] = counts[i] + addition
            spare = spare - addition
    return np.array(counts)


def normal_values(stream_key, dims, deviation, reach, split=(), kind=jnp.bfloat16):
    result = jax.random.normal(stream_key, dims, jnp.float32) * deviation
    if len(split) > 0:
        result = block_levels(stream_key, dims, split, -0.22, 0.18) * result
    return jnp.clip(result, min=-reach, max=reach).astype(kind)


def gaussian_with(rng, shape, width, reach, pieces, heavy, held_as=jnp.bfloat16):
    result = width * jax.random.normal(rng, shape, jnp.float32)
    if pieces:
        result = result * block_levels(rng, shape, pieces, -0.22, 0.18)
    return jnp.clip(raised(result, jax.random.fold_in(rng, 3), *heavy), -reach, reach).astype(held_as)


def setup_inputs(seed: int = 0) -> dict:
    streams_of = jax.random.split(jax.random.key(seed), 7)
    density = jnp.clip(jnp.exp(math.log(2.0) - 1.3862944 * jax.random.uniform(streams_of[0], (ROWS, NT, W), jnp.float32) ** block_levels(streams_of[0], (ROWS, NT, W), ((0, 8), (1, 4)), -0.2, 0.2)), 0.5, 2.0).astype(jnp.bfloat16)
    flow_rest = normal_values(streams_of[1], (ROWS, 4, NT, W), 1.0, 6.0, ((0, 8), (2, 4)))
    dest_keys = jax.random.split(jax.random.fold_in(streams_of[2], 1), ROWS // R_DEV)
    dest_turns = jax.random.permutation(jax.random.fold_in(streams_of[2], 3), ROWS // R_DEV)
    dest = jax.vmap(lambda own, number: routed_block(jax.random.fold_in(streams_of[2], 2), own, number, R_DEV, N_BLK, 1, CAP, 2))(dest_keys, dest_turns).reshape((ROWS, 1))
    weights = gaussian_with(streams_of[3], (N_BLK, NOBS, NT, W), (100 * W * ROWS) ** -0.5, 0.0024414062, ((0, 8), (2, 4)), (0, 1, 8, 2.0))
    directions = normal_values(streams_of[4], (NOBS, 3), 1.0, 4.0, (), jnp.float32)
    bins = place_ends(jax.random.randint(streams_of[5], (NOBS, N_BLK), 0, NT), jax.random.fold_in(streams_of[5], 1), 0, NT - 1).astype(jnp.int32)
    return {"density": density, "flow_rest": flow_rest, "dest": dest, "weights": weights, "directions": directions, "bins": bins}


def stress_parts(rho, flow):
    speed_x = flow[:, 0]
    speed_y = flow[:, 1]
    speed_z = flow[:, 2]
    excess = flow[:, 3]
    return jnp.stack([rho * speed_x * speed_x + excess, rho * speed_y * speed_y + excess,
                      rho * speed_z * speed_z + excess, rho * speed_x * speed_y,
                      rho * speed_x * speed_z, rho * speed_y * speed_z], axis=1)


def reference(density, flow_rest, dest, weights, directions, bins):
    heading = directions
    projector = jnp.stack([heading[:, 0] * heading[:, 0], heading[:, 1] * heading[:, 1],
                           heading[:, 2] * heading[:, 2], 2.0 * heading[:, 0] * heading[:, 1],
                           2.0 * heading[:, 0] * heading[:, 2], 2.0 * heading[:, 1] * heading[:, 2]], axis=1)

    def per_part(running, index):
        start = (index * R_DEV).astype(jnp.int32)
        dens_part = lax.dynamic_slice_in_dim(density, start, R_DEV, 0).astype(jnp.float32)
        flow_part = lax.dynamic_slice_in_dim(flow_rest, start, R_DEV, 0).astype(jnp.float32)
        targets = lax.dynamic_slice_in_dim(dest[:, 0], start, R_DEV, 0)
        stresses = stress_parts(dens_part, flow_part)
        return running + jax.ops.segment_sum(stresses, targets, num_segments=N_BLK), None

    totals, unused = lax.scan(per_part, jnp.zeros((N_BLK, 6, NT, W), jnp.float32),
                              jnp.arange(N_BLK, dtype=jnp.int32))

    def per_block(pair):
        block_totals, block_weights = pair
        moment = jnp.einsum('oi,itc->otc', projector, block_totals, precision=lax.Precision.HIGHEST)
        return jnp.sum(block_weights.astype(jnp.float32) * moment, axis=2)

    source = lax.map(per_block, (totals, weights))
    curved = jnp.roll(source, -1, axis=2) - 2.0 * source + jnp.roll(source, 1, axis=2)
    lagged = jnp.mod(jnp.arange(NT, dtype=jnp.int32)[None, None, :] - jnp.transpose(bins)[:, :, None], NT).astype(jnp.int32)
    shifted = jnp.take_along_axis(curved, lagged, axis=2)
    return jnp.sum(shifted, axis=0)
```

```python
import functools

import jax
import jax.numpy as jnp
from jax import lax
from jax.experimental import pallas as pl
from jax.experimental.pallas import tpu as pltpu
from jax.sharding import PartitionSpec as P

COMPS = 6
TILE = 16
LANES = 128
UNROLL = 4
GRAIN = 128.0
TOP = 32764.0
FLOOR = 1e-35
VMEM_BYTES = 48 * 1024 * 1024


def whole():
    return pl.BlockSpec(memory_space=pltpu.VMEM)


def scalars():
    return pl.BlockSpec(memory_space=pltpu.SMEM)


def params():
    return pltpu.CompilerParams(vmem_limit_bytes=VMEM_BYTES)


def scale_code(largest):
    return jnp.ceil(jnp.log(jnp.maximum(largest, FLOOR)) * GRAIN)


def encode(values, inverse):
    return jnp.round(values * inverse).astype(jnp.int32).astype(jnp.int16)


def encode_factor(code):
    return jnp.exp(code * (-1.0 / GRAIN)) * TOP


def decode_factor(code16):
    code = code16.astype(jnp.int32).astype(jnp.float32)
    return jnp.exp(code * (1.0 / GRAIN)) * (1.0 / TOP)


def decode(code16, factor):
    return code16.astype(jnp.int32).astype(jnp.float32) * factor


def with_bit(index, position, bit):
    low = index & ((1 << position) - 1)
    return ((index >> position) << (position + 1)) | (bit << position) | low


def rows_at(start, size=TILE):
    return pl.ds(pl.multiple_of(start, TILE), size)


def write_codes(largest, staged, send_ref, rows):
    code = scale_code(largest)
    inverse = encode_factor(code)

    def step(k, carry):
        where = rows_at(k * TILE)
        send_ref[where, :] = encode(staged[where, :], inverse)
        return carry

    lax.fori_loop(0, rows // TILE, step, 0, unroll=4)
    send_ref[rows:rows + TILE, :] = code.astype(jnp.int32).astype(jnp.int16)


def stress_kernel(blocks, bits, dest_ref, density_ref, flow_ref, *refs):
    halves = len(bits)
    sends, keeps = refs[:halves], refs[halves:2 * halves]
    dens, flow, staged, counts, members, sems = refs[2 * halves:]
    rows, steps = density_ref.shape[0], density_ref.shape[1]
    tiles = steps // TILE
    per_half = tiles // halves
    span = steps // halves
    copies = []
    for k in range(tiles):
        at = pl.ds(k * TILE, TILE)
        copies.append((
            pltpu.make_async_copy(density_ref.at[:, at, :], dens.at[pl.ds(0, rows), at, :], sems.at[k, 0]),
            pltpu.make_async_copy(flow_ref.at[:, :, at, :], flow.at[pl.ds(0, rows), :, at, :], sems.at[k, 1]),
        ))
    for pair in copies:
        for copy in pair:
            copy.start()

    dens[rows] = jnp.zeros_like(dens[rows])
    flow[rows] = jnp.zeros_like(flow[rows])
    stride = rows + UNROLL

    def clear(b, carry):
        counts[b] = 0
        return carry

    lax.fori_loop(0, blocks, clear, 0)

    def place(r, carry):
        target = dest_ref[r]
        count = counts[target]
        members[target * stride + count] = r
        counts[target] = count + 1
        return carry

    lax.fori_loop(0, rows, place, 0, unroll=4)

    def pad(b, carry):
        end = b * stride + counts[b]
        for extra in range(UNROLL - 1):
            members[end + extra] = rows
        return carry

    lax.fori_loop(0, blocks, pad, 0)

    me = lax.axis_index("blk")

    def sums(slot, at):
        target = me ^ slot
        first = target * stride

        def body(turn, totals):
            totals = list(totals)
            for u in range(UNROLL):
                row = members[first + turn * UNROLL + u]
                rho = dens[row, at, :].astype(jnp.float32)
                ux = flow[row, 0, at, :].astype(jnp.float32)
                uy = flow[row, 1, at, :].astype(jnp.float32)
                uz = flow[row, 2, at, :].astype(jnp.float32)
                excess = flow[row, 3, at, :].astype(jnp.float32)
                mx, my, mz = rho * ux, rho * uy, rho * uz
                for i, term in enumerate((mx * ux, my * uy, mz * uz, mx * uy, mx * uz, my * uz, excess)):
                    totals[i] = totals[i] + term
            return tuple(totals)

        zero = jnp.zeros((TILE, LANES), jnp.float32)
        turns = (counts[target] + (UNROLL - 1)) // UNROLL
        xx, yy, zz, xy, xz, yz, excess = lax.fori_loop(0, turns, body, (zero,) * 7)
        return xx + excess, yy + excess, zz + excess, xy, xz, yz

    for half in range(halves):
        largest = jnp.zeros((TILE, LANES), jnp.float32)
        for k in range(per_half):
            tile = half * per_half + k
            at = slice(tile * TILE, (tile + 1) * TILE)
            for copy in copies[tile]:
                copy.wait()

            def sent(i, top):
                pieces = sums(with_bit(i, bits[half], 1), at)
                for c, piece in enumerate(pieces):
                    staged[rows_at((i * COMPS + c) * span + k * TILE), :] = piece
                    top = jnp.maximum(top, jnp.abs(piece))
                return top

            largest = lax.fori_loop(0, blocks // 2, sent, largest)

            def kept(i, carry):
                pieces = sums(with_bit(i, bits[half], 0), at)
                for c, piece in enumerate(pieces):
                    keeps[half][rows_at((i * COMPS + c) * span + k * TILE), :] = piece
                return carry

            lax.fori_loop(0, blocks // 2, kept, 0)
        write_codes(largest, staged, sends[half], blocks // 2 * COMPS * span)


def stress_sums(density, flow_rest, targets, blocks, bits):
    rows, steps, _ = density.shape
    halves = len(bits)
    sent = blocks // 2 * COMPS * (steps // halves)
    outs = [jax.ShapeDtypeStruct((sent + TILE, LANES), jnp.int16)] * halves
    outs += [jax.ShapeDtypeStruct((sent, LANES), jnp.float32)] * halves
    got = pl.pallas_call(
        functools.partial(stress_kernel, blocks, bits),
        out_shape=outs,
        in_specs=[scalars(), pl.BlockSpec(memory_space=pl.ANY), pl.BlockSpec(memory_space=pl.ANY)],
        out_specs=[whole()] * len(outs),
        scratch_shapes=[
            pltpu.VMEM((rows + 1, steps, LANES), density.dtype),
            pltpu.VMEM((rows + 1, flow_rest.shape[1], steps, LANES), flow_rest.dtype),
            pltpu.VMEM((sent, LANES), jnp.float32),
            pltpu.SMEM((blocks,), jnp.int32),
            pltpu.SMEM((blocks * (rows + UNROLL),), jnp.int32),
            pltpu.SemaphoreType.DMA((steps // TILE, 2)),
        ],
        compiler_params=params(),
        name="stress_sums",
    )(targets, density, flow_rest)
    return got[:halves], got[halves:]


def merge_kernel(count, position, block_rows, joined, *refs):
    pieces = len(block_rows)
    groups = 1 if joined else pieces
    got, kept = refs[:pieces], refs[pieces:2 * pieces]
    sends, keeps = refs[2 * pieces:2 * pieces + groups], refs[2 * pieces + groups:2 * pieces + 2 * groups]
    staged = refs[-1]
    half = count // 2
    largest = jnp.zeros((TILE, LANES), jnp.float32)
    for p in range(pieces):
        size = block_rows[p]
        group = 0 if joined else p
        pitch = sum(block_rows) if joined else size
        offset = sum(block_rows[:p]) if joined else 0
        factor = decode_factor(got[p][count * size:count * size + TILE, :])
        if not joined:
            largest = jnp.zeros((TILE, LANES), jnp.float32)

        def total(block, k):
            where = rows_at(block * size + k * TILE)
            return kept[p][where, :] + decode(got[p][where, :], factor)

        def sent(i, top):
            def tile(k, top):
                piece = total(with_bit(i, position[p], 1), k)
                staged[rows_at(i * pitch + offset + k * TILE), :] = piece
                return jnp.maximum(top, jnp.abs(piece))

            return lax.fori_loop(0, size // TILE, tile, top, unroll=4)

        largest = lax.fori_loop(0, half, sent, largest)

        def stay(i, carry):
            def tile(k, carry):
                keeps[group][rows_at(i * pitch + offset + k * TILE), :] = total(with_bit(i, position[p], 0), k)
                return carry

            return lax.fori_loop(0, size // TILE, tile, carry, unroll=4)

        lax.fori_loop(0, half, stay, 0)
        if not joined or p == pieces - 1:
            write_codes(largest, staged, sends[group], half * pitch)


def merge(got, kept, count, position, block_rows, joined):
    half = count // 2
    pitches = [sum(block_rows)] if joined else list(block_rows)
    outs = [jax.ShapeDtypeStruct((half * pitch + TILE, LANES), jnp.int16) for pitch in pitches]
    outs += [jax.ShapeDtypeStruct((half * pitch, LANES), jnp.float32) for pitch in pitches]
    made = pl.pallas_call(
        functools.partial(merge_kernel, count, tuple(position), tuple(block_rows), joined),
        out_shape=outs,
        in_specs=[whole()] * (2 * len(got)),
        out_specs=[whole()] * len(outs),
        scratch_shapes=[pltpu.VMEM((half * max(pitches), LANES), jnp.float32)],
        compiler_params=params(),
        name="merge",
    )(*got, *kept)
    return made[:len(pitches)], made[len(pitches):]


def source_kernel(halves, per_device, copies, proj_ref, got_ref, kept_ref, weights_ref, out_ref, totals, source):
    observers, steps, _ = weights_ref.shape
    span = steps // halves
    factor = decode_factor(got_ref[COMPS * steps:COMPS * steps + TILE, :])

    def fill(k, carry):
        where = rows_at(k * TILE)
        totals[where, :] = kept_ref[where, :] + decode(got_ref[where, :], factor)
        return carry

    lax.fori_loop(0, COMPS * steps // TILE, fill, 0, unroll=4)
    lane = lax.broadcasted_iota(jnp.int32, (TILE, LANES), 1)

    def times(tile, carry):
        half = tile // (span // TILE)
        inside = tile - half * (span // TILE)
        parts = [totals[rows_at((half * COMPS + c) * span + inside * TILE), :] for c in range(COMPS)]

        def weighted(o):
            moment = proj_ref[o * COMPS] * parts[0]
            for c in range(1, COMPS):
                moment = moment + proj_ref[o * COMPS + c] * parts[c]
            return weights_ref[o, rows_at(tile * TILE), :].astype(jnp.float32) * moment

        def summed(first, number):
            if number == 1:
                return weighted(first)
            step = number // 2
            return join(first, number, step)

        def join(first, number, step):
            even = summed_at(first, number, 0)
            odd = summed_at(first, number, step)
            clear = (lane & step) == 0
            return jnp.where(clear, even, odd) + pltpu.roll(jnp.where(clear, odd, even), step, 1)

        def summed_at(first, number, extra):
            return summed(first + extra, number // 2)

        value = summed(0, observers)
        width = observers
        while width < LANES:
            value = value + pltpu.roll(value, width, 1)
            width *= 2
        source[rows_at(tile * TILE), :] = value
        source[rows_at(steps + tile * TILE), :] = value
        return carry

    lax.fori_loop(0, steps // TILE, times, 0)
    across = source[...].T
    if per_device % 2 == 0:
        half = per_device // 2
        lanes = lax.broadcasted_iota(jnp.int32, (per_device, LANES), 1)
        for b in range(observers // per_device):
            mine = across[b * per_device:(b + 1) * per_device]
            packed = jnp.where(lanes < steps, mine, jnp.concatenate([mine[half:], mine[:half]], axis=0))[:half]
            for copy in range(copies):
                out_ref[b * copies + copy] = packed
    else:
        for b in range(observers // per_device):
            for copy in range(copies):
                out_ref[b * copies + copy] = across[b * per_device:(b + 1) * per_device]


def sources(projector, got, kept, weights, halves, blocks, copies):
    observers, steps, _ = weights.shape
    per_device = observers // blocks
    rows = per_device // 2 if per_device % 2 == 0 else per_device
    return pl.pallas_call(
        functools.partial(source_kernel, halves, per_device, copies),
        out_shape=jax.ShapeDtypeStruct((blocks * copies, rows, LANES), jnp.float32),
        in_specs=[scalars()] + [whole()] * 3,
        out_specs=whole(),
        scratch_shapes=[
            pltpu.VMEM((COMPS * steps, LANES), jnp.float32),
            pltpu.VMEM((2 * steps, LANES), jnp.float32),
        ],
        compiler_params=params(),
        name="sources",
    )(projector, got, kept, weights)


def record_kernel(blocks, slabs, steps, got_ref, delay_ref, out_ref):
    per_device = out_ref.shape[0]
    period = slabs * steps
    lanes = lax.broadcasted_iota(jnp.int32, (per_device, LANES), 1)
    row = lax.broadcasted_iota(jnp.int32, (per_device, LANES), 0)
    packed = per_device % 2 == 0

    def unpacked(chunk):
        if not packed:
            return chunk, chunk
        both = jnp.concatenate([chunk, chunk], axis=0)
        turned = pltpu.roll(both, steps, 1)
        upper = row < per_device // 2
        return jnp.where(upper, both, turned), jnp.where(upper, turned, both)

    pieces, delays = [], []
    for b in range(blocks):
        columns = []
        for s in range(0, slabs, 2):
            low, _ = unpacked(got_ref[b * slabs + s])
            _, high = unpacked(got_ref[b * slabs + s + 1])
            columns.append(jnp.where(lanes < steps, low, high))
        pieces.append(jnp.concatenate(columns, axis=1))
        delays.append(delay_ref[b * slabs])
    value = jnp.concatenate(pieces, axis=0)
    delay = jnp.concatenate(delays, axis=0)
    delay = delay - lax.axis_index("tm") * steps
    delay = jnp.where(delay < 0, delay + period, delay)
    delay = jnp.concatenate([delay] * (period // LANES), axis=1)
    shift = 1
    while shift < period:
        value = jnp.where((delay & shift) != 0, pltpu.roll(value, shift, 1), value)
        shift *= 2
    total = value[:per_device]
    for b in range(1, blocks):
        total = total + value[b * per_device:(b + 1) * per_device]
    curved = pltpu.roll(total, period - 1, 1) - 2.0 * total + pltpu.roll(total, 1, 1)
    out_ref[...] = curved[:, :steps]


def records(got, delays, blocks, slabs, steps, per_device):
    return pl.pallas_call(
        functools.partial(record_kernel, blocks, slabs, steps),
        out_shape=jax.ShapeDtypeStruct((per_device, steps), jnp.float32),
        in_specs=[whole()] * 2,
        out_specs=whole(),
        compiler_params=params(),
        name="records",
    )(got, delays)


def body(density, flow_rest, dest, weights, directions, bins):
    blocks, slabs = lax.axis_size("blk"), lax.axis_size("tm")
    steps = density.shape[1]
    observers = bins.shape[0]
    per_device = observers // blocks

    def swap(values, bit):
        return lax.ppermute(values, "blk", [(i, i ^ (1 << bit)) for i in range(blocks)])

    orders = ((0, 1), (1, 0))
    (send_a, send_b), (keep_a, keep_b) = stress_sums(
        density, flow_rest, dest[:, 0], blocks, tuple(order[0] for order in orders)
    )
    span_rows = COMPS * (steps // 2)
    got = [swap(send_a, 0), swap(send_b, 1)]

    delays = jnp.broadcast_to(
        bins.reshape(blocks, 1, per_device, 1), (blocks, slabs, per_device, LANES)
    ).reshape(blocks * slabs, per_device, LANES)
    delays = lax.all_to_all(delays, ("blk", "tm"), split_axis=0, concat_axis=0, tiled=True)

    count = blocks // 2
    (send_a, send_b), (keep_a, keep_b) = merge(
        got, [keep_a, keep_b], count, [0, 0], [span_rows, span_rows], False
    )
    got = [swap(send_a, 1), swap(send_b, 0)]
    count //= 2
    kept, sizes, joined, bit = [keep_a, keep_b], [span_rows, span_rows], True, 2
    while count > 1:
        (send,), (keep,) = merge(got, kept, count, [0] * len(got), sizes, joined)
        got, kept, sizes = [swap(send, bit)], [keep], [2 * span_rows]
        count //= 2
        bit += 1

    d1, d2, d3 = directions[:, 0], directions[:, 1], directions[:, 2]
    projector = jnp.stack(
        [d1 * d1, d2 * d2, d3 * d3, 2.0 * d1 * d2, 2.0 * d1 * d3, 2.0 * d2 * d3], axis=1
    ).reshape(observers * COMPS)
    chunks = sources(projector, got[0], kept[0], weights[0], 2, blocks, slabs)
    chunks = lax.all_to_all(chunks, ("blk", "tm"), split_axis=0, concat_axis=0, tiled=True)
    return records(chunks, delays, blocks, slabs, steps, per_device)


def solution(mesh):
    placed = (
        P("blk", "tm", None),
        P("blk", None, "tm", None),
        P("blk", None),
        P("blk", None, "tm", None),
        P(),
        P(None, "blk"),
    )
    return jax.shard_map(
        body, mesh=mesh, in_specs=placed, out_specs=P("blk", "tm"), check_vma=False
    )
```

```python
import functools

import jax
import jax.numpy as jnp
from jax import lax
from jax.experimental import pallas as pl
from jax.experimental.pallas import tpu as pltpu
from jax.sharding import PartitionSpec as P

COMPS = 6
TILE = 16
LANES = 128
GROUP = 8
UNROLL = 4
GRAIN = 128.0
TOP = 32764.0
FLOOR = 1e-35


def whole():
    return pl.BlockSpec(memory_space=pltpu.VMEM)


def scalars():
    return pl.BlockSpec(memory_space=pltpu.SMEM)


def params(mebibytes=40):
    return pltpu.CompilerParams(vmem_limit_bytes=mebibytes * 1024 * 1024)


def scale_code(largest):
    return jnp.ceil(jnp.log(jnp.maximum(largest, FLOOR)) * GRAIN)


def encode(values, inverse):
    return jnp.round(values * inverse).astype(jnp.int32).astype(jnp.int16)


def encode_factor(code):
    return jnp.exp(code * (-1.0 / GRAIN)) * TOP


def decode_factor(code16):
    code = code16.astype(jnp.int32).astype(jnp.float32)
    return jnp.exp(code * (1.0 / GRAIN)) * (1.0 / TOP)


def decode(code16, factor):
    return code16.astype(jnp.int32).astype(jnp.float32) * factor


def with_bit(index, position, bit):
    low = index & ((1 << position) - 1)
    return ((index >> position) << (position + 1)) | (bit << position) | low


def rows_at(start, size=TILE):
    return pl.ds(pl.multiple_of(start, TILE), size)


def write_codes(largest, staged, send_ref, rows):
    code = scale_code(largest)
    inverse = encode_factor(code)

    def step(k, carry):
        where = rows_at(k * TILE)
        send_ref[where, :] = encode(staged[where, :], inverse)
        return carry

    lax.fori_loop(0, rows // TILE, step, 0, unroll=4)
    send_ref[rows:rows + TILE, :] = code.astype(jnp.int32).astype(jnp.int16)


def bucket(blocks, rows, dest_ref, counts, members):
    stride = rows + UNROLL

    def clear(b, carry):
        counts[b] = 0
        return carry

    lax.fori_loop(0, blocks, clear, 0)

    def place(r, carry):
        target = dest_ref[r]
        count = counts[target]
        members[target * stride + count] = r
        counts[target] = count + 1
        return carry

    lax.fori_loop(0, rows, place, 0, unroll=4)

    def pad(b, carry):
        end = b * stride + counts[b]
        for extra in range(UNROLL - 1):
            members[end + extra] = rows
        return carry

    lax.fori_loop(0, blocks, pad, 0)


def block_sums(target, at, stride, dens, flow, counts, members):
    first = target * stride

    def body(turn, totals):
        totals = list(totals)
        for u in range(UNROLL):
            row = members[first + turn * UNROLL + u]
            rho = dens[row, at, :].astype(jnp.float32)
            ux = flow[row, 0, at, :].astype(jnp.float32)
            uy = flow[row, 1, at, :].astype(jnp.float32)
            uz = flow[row, 2, at, :].astype(jnp.float32)
            excess = flow[row, 3, at, :].astype(jnp.float32)
            mx, my, mz = rho * ux, rho * uy, rho * uz
            for i, term in enumerate((mx * ux, my * uy, mz * uz, mx * uy, mx * uz, my * uz, excess)):
                totals[i] = totals[i] + term
        return tuple(totals)

    zero = jnp.zeros((TILE, LANES), jnp.float32)
    turns = (counts[target] + (UNROLL - 1)) // UNROLL
    xx, yy, zz, xy, xz, yz, excess = lax.fori_loop(0, turns, body, (zero,) * 7)
    return xx + excess, yy + excess, zz + excess, xy, xz, yz


def stress_kernel(blocks, bits, leaving, dest_ref, density_ref, flow_ref, *refs):
    halves = len(bits)
    outs, (dens, flow, dest, counts, members, staged, sems, dest_sem) = refs[:halves], refs[halves:]
    rows, steps = density_ref.shape[0], density_ref.shape[1]
    tiles = steps // TILE
    per_half = tiles // halves
    span = steps // halves
    fetch = pltpu.make_async_copy(dest_ref, dest, dest_sem)
    fetch.start()
    copies = []
    for k in range(tiles):
        at = pl.ds(k * TILE, TILE)
        pair = (
            pltpu.make_async_copy(density_ref.at[:, at, :], dens.at[pl.ds(0, rows), at, :], sems.at[k, 0]),
            pltpu.make_async_copy(flow_ref.at[:, :, at, :], flow.at[pl.ds(0, rows), :, at, :], sems.at[k, 1]),
        )
        for copy in pair:
            copy.start()
        copies.append(pair)

    dens[rows] = jnp.zeros_like(dens[rows])
    flow[rows] = jnp.zeros_like(flow[rows])
    fetch.wait()
    bucket(blocks, rows, dest, counts, members)
    me = lax.axis_index("blk")
    for half in range(halves):
        target_ref = staged if leaving else outs[half]
        largest = jnp.zeros((TILE, LANES), jnp.float32)
        for k in range(per_half):
            tile = half * per_half + k
            at = slice(tile * TILE, (tile + 1) * TILE)
            for copy in copies[tile]:
                copy.wait()

            def block(i, top):
                target = me ^ with_bit(i, bits[half], int(leaving))
                pieces = block_sums(target, at, rows + UNROLL, dens, flow, counts, members)
                for c, piece in enumerate(pieces):
                    target_ref[rows_at((i * COMPS + c) * span + k * TILE), :] = piece
                    if leaving:
                        top = jnp.maximum(top, jnp.abs(piece))
                return top

            largest = lax.fori_loop(0, blocks // 2, block, largest)
        if leaving:
            write_codes(largest, staged, outs[half], blocks // 2 * COMPS * span)


def stress_sums(density, flow_rest, targets, blocks, bits, leaving):
    rows, steps, _ = density.shape
    halves = len(bits)
    size = blocks // 2 * COMPS * (steps // halves)
    if leaving:
        out = jax.ShapeDtypeStruct((size + TILE, LANES), jnp.int16)
    else:
        out = jax.ShapeDtypeStruct((size, LANES), jnp.float32)
    return pl.pallas_call(
        functools.partial(stress_kernel, blocks, bits, leaving),
        out_shape=[out] * halves,
        in_specs=[pl.BlockSpec(memory_space=pl.ANY)] * 3,
        out_specs=[whole()] * halves,
        scratch_shapes=[
            pltpu.VMEM((rows + 1, steps, LANES), density.dtype),
            pltpu.VMEM((rows + 1, flow_rest.shape[1], steps, LANES), flow_rest.dtype),
            pltpu.SMEM((rows,), jnp.int32),
            pltpu.SMEM((blocks,), jnp.int32),
            pltpu.SMEM((blocks * (rows + UNROLL),), jnp.int32),
            pltpu.VMEM((size if leaving else TILE, LANES), jnp.float32),
            pltpu.SemaphoreType.DMA((steps // TILE, 2)),
            pltpu.SemaphoreType.DMA(()),
        ],
        compiler_params=params(58 if leaving else 50),
        name="leaving_sums" if leaving else "staying_sums",
    )(targets, density, flow_rest)


def merge_kernel(count, positions, size, messages, *refs):
    halves = len(positions)
    got, kept = refs[:messages], refs[messages:messages + halves]
    send, keeps, staged = refs[messages + halves], refs[messages + halves + 1:-1], refs[-1]
    half = count // 2
    largest = jnp.zeros((TILE, LANES), jnp.float32)
    for p in range(halves):
        message = got[min(p, messages - 1)]
        offset = (p if messages < halves else 0) * count * size
        factor = decode_factor(message[message.shape[0] - TILE:, :])

        def total(block, k):
            where = block * size + k * TILE
            return kept[p][rows_at(where), :] + decode(message[rows_at(offset + where), :], factor)

        def sent(i, top):
            def tile(k, top):
                piece = total(with_bit(i, positions[p], 1), k)
                staged[rows_at((p * half + i) * size + k * TILE), :] = piece
                return jnp.maximum(top, jnp.abs(piece))

            return lax.fori_loop(0, size // TILE, tile, top, unroll=4)

        largest = lax.fori_loop(0, half, sent, largest)

        def stay(i, carry):
            def tile(k, carry):
                keeps[p][rows_at(i * size + k * TILE), :] = total(with_bit(i, positions[p], 0), k)
                return carry

            return lax.fori_loop(0, size // TILE, tile, carry, unroll=4)

        lax.fori_loop(0, half, stay, 0)
    write_codes(largest, staged, send, halves * half * size)


def merge(got, kept, count, positions, size):
    rows = count // 2 * size
    halves = len(kept)
    made = pl.pallas_call(
        functools.partial(merge_kernel, count, tuple(positions), size, len(got)),
        out_shape=[jax.ShapeDtypeStruct((halves * rows + TILE, LANES), jnp.int16)]
        + [jax.ShapeDtypeStruct((rows, LANES), jnp.float32)] * halves,
        in_specs=[whole()] * (len(got) + halves),
        out_specs=[whole()] * (1 + halves),
        scratch_shapes=[pltpu.VMEM((halves * rows, LANES), jnp.float32)],
        compiler_params=params(),
        name="merge",
    )(*got, *kept)
    return made[0], list(made[1:])


def project(half, got_ref, kept_ref, proj_ref, weights_ref, totals):
    observers = weights_ref.shape[0]
    span = kept_ref.shape[0] // COMPS
    factor = decode_factor(got_ref[COMPS * span:COMPS * span + TILE, :])

    def fill(k, carry):
        where = rows_at(k * TILE)
        totals[where, :] = kept_ref[where, :] + decode(got_ref[where, :], factor)
        return carry

    lax.fori_loop(0, COMPS * span // TILE, fill, 0, unroll=4)
    lane = lax.broadcasted_iota(jnp.int32, (span, LANES), 1) % observers
    ones = jnp.ones((2 * LANES, LANES), jnp.bfloat16)
    at = slice(half * span, (half + 1) * span)
    parts = [totals[c * span:(c + 1) * span, :] for c in range(COMPS)]
    value = jnp.zeros((span, LANES), jnp.float32)
    for group in range(0, observers, GROUP):
        rows = []
        for o in range(group, group + GROUP):
            moment = proj_ref[o:o + 1, :] * parts[0]
            for c in range(1, COMPS):
                moment = moment + proj_ref[c * observers + o:c * observers + o + 1, :] * parts[c]
            term = weights_ref[o, at, :].astype(jnp.float32) * moment
            high = term.astype(jnp.bfloat16)
            low = (term - high.astype(jnp.float32)).astype(jnp.bfloat16)
            rows.append(jnp.concatenate([high, low], axis=1))
        sums = jnp.dot(jnp.concatenate(rows, axis=0), ones, preferred_element_type=jnp.float32)
        for u in range(GROUP):
            value = jnp.where(lane == group + u, sums[u * span:(u + 1) * span], value)
    return value


def first_kernel(proj_ref, got_ref, kept_ref, weights_ref, out_ref, totals):
    out_ref[...] = project(0, got_ref, kept_ref, proj_ref, weights_ref, totals)


def last_kernel(slabs, per_device, proj_ref, got_ref, kept_ref, weights_ref, first_ref, bins_ref, out_ref, totals):
    observers, steps, _ = weights_ref.shape
    source = jnp.concatenate(
        [first_ref[...], project(1, got_ref, kept_ref, proj_ref, weights_ref, totals)], axis=0
    )
    across = jnp.concatenate([source] * (LANES // steps), axis=0).T[:observers]
    period = slabs * steps
    lane = lax.broadcasted_iota(jnp.int32, (observers, LANES), 1)
    blank = jnp.zeros((observers, LANES), jnp.float32)
    value = jnp.concatenate([jnp.where(lane < steps, across, blank)] + [blank] * (period // LANES - 1), axis=1)
    value = pltpu.roll(value, period - 1, 1) - 2.0 * value + pltpu.roll(value, 1, 1)
    delay = bins_ref[...] + lax.axis_index("tm") * steps
    delay = jnp.where(delay >= period, delay - period, delay)
    shift = 1
    while shift < period:
        value = jnp.where((delay & shift) != 0, pltpu.roll(value, shift, 1), value)
        shift *= 2
    rows = out_ref.shape[1]
    lane = lax.broadcasted_iota(jnp.int32, (per_device, LANES), 1)
    low = lane < steps
    for b in range(observers // per_device):
        for pair in range(period // LANES):
            mine = value[b * per_device:(b + 1) * per_device, pair * LANES:(pair + 1) * LANES]
            turned = pltpu.roll(mine, steps, 1)
            if rows < per_device:
                down = jnp.concatenate([mine[rows:], mine[:rows]], axis=0)
                down_turned = jnp.concatenate([turned[rows:], turned[:rows]], axis=0)
                out_ref[b * slabs + 2 * pair] = jnp.where(low, mine, down_turned)[:rows]
                out_ref[b * slabs + 2 * pair + 1] = jnp.where(low, turned, down)[:rows]
            else:
                out_ref[b * slabs + 2 * pair] = mine
                out_ref[b * slabs + 2 * pair + 1] = turned


def sources(projector, got, kept, weights, bins, blocks, slabs):
    observers = weights.shape[0]
    per_device = observers // blocks
    rows = per_device // 2 if per_device % 2 == 0 else per_device
    size = kept[0].shape[0]
    first = pl.pallas_call(
        first_kernel,
        out_shape=jax.ShapeDtypeStruct((size // COMPS, LANES), jnp.float32),
        in_specs=[whole()] * 4,
        out_specs=whole(),
        scratch_shapes=[pltpu.VMEM((size, LANES), jnp.float32)],
        compiler_params=params(),
        name="first_sources",
    )(projector, got[0], kept[0], weights)
    return pl.pallas_call(
        functools.partial(last_kernel, slabs, per_device),
        out_shape=jax.ShapeDtypeStruct((blocks * slabs, rows, LANES), jnp.float32),
        in_specs=[whole()] * 6,
        out_specs=whole(),
        scratch_shapes=[pltpu.VMEM((size, LANES), jnp.float32)],
        compiler_params=params(),
        name="last_sources",
    )(projector, got[1], kept[1], weights, first, bins)


def record_kernel(got_ref, out_ref):
    per_device, steps = out_ref.shape
    total = got_ref[0]
    for k in range(1, got_ref.shape[0]):
        total = total + got_ref[k]
    rows = total.shape[0]
    out_ref[:rows, :] = total[:, :steps]
    if rows < per_device:
        out_ref[rows:, :] = total[:, steps:]


def records(got, per_device, steps):
    return pl.pallas_call(
        record_kernel,
        out_shape=jax.ShapeDtypeStruct((per_device, steps), jnp.float32),
        in_specs=[whole()],
        out_specs=whole(),
        compiler_params=params(),
        name="records",
    )(got)


def body(density, flow_rest, dest, weights, directions, bins):
    blocks, slabs = lax.axis_size("blk"), lax.axis_size("tm")
    steps = density.shape[1]
    observers = bins.shape[0]

    def swap(values, bit):
        return lax.ppermute(values, "blk", [(i, i ^ (1 << bit)) for i in range(blocks)])

    stages = blocks.bit_length() - 1
    orders = [list(range(stages)) for _ in range(2)]
    orders[1][:2] = [1, 0]
    size = COMPS * (steps // 2)
    bits = tuple(order[0] for order in orders)
    sends = stress_sums(density, flow_rest, dest[:, 0], blocks, bits, True)
    kept = stress_sums(density, flow_rest, dest[:, 0], blocks, bits, False)
    got = [swap(send, order[0]) for send, order in zip(sends, orders)]
    count = blocks // 2
    for stage in range(1, stages):
        places = [sorted(order[stage:]).index(order[stage]) for order in orders]
        made = [merge(got[p:p + 1], kept[p:p + 1], count, places[p:p + 1], size) for p in range(2)]
        got = [swap(made[p][0], orders[p][stage]) for p in range(2)]
        kept = made[0][1] + made[1][1]
        count //= 2

    d1, d2, d3 = [jnp.broadcast_to(directions[:, c:c + 1], (observers, LANES)) for c in range(3)]
    projector = jnp.concatenate(
        [d1 * d1, d2 * d2, d3 * d3, 2.0 * d1 * d2, 2.0 * d1 * d3, 2.0 * d2 * d3], axis=0
    )
    chunks = sources(projector, got, kept, weights[0], bins, blocks, slabs)
    chunks = lax.all_to_all(chunks, ("blk", "tm"), split_axis=0, concat_axis=0, tiled=True)
    return records(chunks, observers // blocks, steps)


def solution(mesh):
    placed = (
        P("blk", "tm", None),
        P("blk", None, "tm", None),
        P("blk", None),
        P("blk", None, "tm", None),
        P(),
        P(None, "blk"),
    )
    return jax.shard_map(
        body, mesh=mesh, in_specs=placed, out_specs=P("blk", "tm"), check_vma=False
    )
```

```python
import functools

import jax
import jax.numpy as jnp
from jax import lax
from jax.experimental import pallas as pl
from jax.experimental.pallas import tpu as pltpu
from jax.sharding import PartitionSpec as P

COMPS = 6
TILE = 16
LANES = 128
GROUP = 8
UNROLL = 4
GRAIN = 128.0
TOP = 32764.0
FLOOR = 1e-35


def whole():
    return pl.BlockSpec(memory_space=pltpu.VMEM)


def scalars():
    return pl.BlockSpec(memory_space=pltpu.SMEM)


def params(mebibytes=40):
    return pltpu.CompilerParams(vmem_limit_bytes=mebibytes * 1024 * 1024)


def scale_code(largest):
    return jnp.ceil(jnp.log(jnp.maximum(largest, FLOOR)) * GRAIN)


def encode(values, inverse):
    return jnp.round(values * inverse).astype(jnp.int32).astype(jnp.int16)


def encode_factor(code):
    return jnp.exp(code * (-1.0 / GRAIN)) * TOP


def decode_factor(code16):
    code = code16.astype(jnp.int32).astype(jnp.float32)
    return jnp.exp(code * (1.0 / GRAIN)) * (1.0 / TOP)


def decode(code16, factor):
    return code16.astype(jnp.int32).astype(jnp.float32) * factor


def with_bit(index, position, bit):
    low = index & ((1 << position) - 1)
    return ((index >> position) << (position + 1)) | (bit << position) | low


def rows_at(start, size=TILE):
    return pl.ds(pl.multiple_of(start, TILE), size)


def write_codes(largest, staged, send_ref, rows):
    code = scale_code(largest)
    inverse = encode_factor(code)

    def step(k, carry):
        where = rows_at(k * TILE)
        send_ref[where, :] = encode(staged[where, :], inverse)
        return carry

    lax.fori_loop(0, rows // TILE, step, 0, unroll=4)
    send_ref[rows:rows + TILE, :] = code.astype(jnp.int32).astype(jnp.int16)


def bucket(blocks, rows, dest_ref, counts, members):
    stride = rows + UNROLL

    def clear(b, carry):
        counts[b] = 0
        return carry

    lax.fori_loop(0, blocks, clear, 0)

    def place(r, carry):
        target = dest_ref[r]
        count = counts[target]
        members[target * stride + count] = r
        counts[target] = count + 1
        return carry

    lax.fori_loop(0, rows, place, 0, unroll=4)

    def pad(b, carry):
        end = b * stride + counts[b]
        for extra in range(UNROLL - 1):
            members[end + extra] = rows
        return carry

    lax.fori_loop(0, blocks, pad, 0)


def block_sums(target, at, stride, dens, flow, counts, members):
    first = target * stride

    def body(turn, totals):
        totals = list(totals)
        for u in range(UNROLL):
            row = members[first + turn * UNROLL + u]
            rho = dens[row, at, :].astype(jnp.float32)
            ux = flow[row, 0, at, :].astype(jnp.float32)
            uy = flow[row, 1, at, :].astype(jnp.float32)
            uz = flow[row, 2, at, :].astype(jnp.float32)
            excess = flow[row, 3, at, :].astype(jnp.float32)
            mx, my, mz = rho * ux, rho * uy, rho * uz
            for i, term in enumerate((mx * ux, my * uy, mz * uz, mx * uy, mx * uz, my * uz, excess)):
                totals[i] = totals[i] + term
        return tuple(totals)

    zero = jnp.zeros((TILE, LANES), jnp.float32)
    turns = (counts[target] + (UNROLL - 1)) // UNROLL
    xx, yy, zz, xy, xz, yz, excess = lax.fori_loop(0, turns, body, (zero,) * 7)
    return xx + excess, yy + excess, zz + excess, xy, xz, yz


def stress_kernel(blocks, bits, leaving, dest_ref, density_ref, flow_ref, *refs):
    halves = len(bits)
    outs, (dens, flow, dest, counts, members, staged, sems, dest_sem) = refs[:halves], refs[halves:]
    rows, steps = density_ref.shape[0], density_ref.shape[1]
    tiles = steps // TILE
    per_half = tiles // halves
    span = steps // halves
    fetch = pltpu.make_async_copy(dest_ref, dest, dest_sem)
    fetch.start()
    copies = []
    for k in range(tiles):
        at = pl.ds(k * TILE, TILE)
        pair = (
            pltpu.make_async_copy(density_ref.at[:, at, :], dens.at[pl.ds(0, rows), at, :], sems.at[k, 0]),
            pltpu.make_async_copy(flow_ref.at[:, :, at, :], flow.at[pl.ds(0, rows), :, at, :], sems.at[k, 1]),
        )
        for copy in pair:
            copy.start()
        copies.append(pair)

    dens[rows] = jnp.zeros_like(dens[rows])
    flow[rows] = jnp.zeros_like(flow[rows])
    fetch.wait()
    bucket(blocks, rows, dest, counts, members)
    me = lax.axis_index("blk")
    for half in range(halves):
        target_ref = staged if leaving else outs[half]
        largest = jnp.zeros((TILE, LANES), jnp.float32)
        for k in range(per_half):
            tile = half * per_half + k
            at = slice(tile * TILE, (tile + 1) * TILE)
            for copy in copies[tile]:
                copy.wait()

            def block(i, top):
                target = me ^ with_bit(i, bits[half], int(leaving))
                pieces = block_sums(target, at, rows + UNROLL, dens, flow, counts, members)
                for c, piece in enumerate(pieces):
                    target_ref[rows_at((i * COMPS + c) * span + k * TILE), :] = piece
                    if leaving:
                        top = jnp.maximum(top, jnp.abs(piece))
                return top

            largest = lax.fori_loop(0, blocks // 2, block, largest)
        if leaving:
            write_codes(largest, staged, outs[half], blocks // 2 * COMPS * span)


def stress_sums(density, flow_rest, targets, blocks, bits, leaving):
    rows, steps, _ = density.shape
    halves = len(bits)
    size = blocks // 2 * COMPS * (steps // halves)
    if leaving:
        out = jax.ShapeDtypeStruct((size + TILE, LANES), jnp.int16)
    else:
        out = jax.ShapeDtypeStruct((size, LANES), jnp.float32)
    return pl.pallas_call(
        functools.partial(stress_kernel, blocks, bits, leaving),
        out_shape=[out] * halves,
        in_specs=[pl.BlockSpec(memory_space=pl.ANY)] * 3,
        out_specs=[whole()] * halves,
        scratch_shapes=[
            pltpu.VMEM((rows + 1, steps, LANES), density.dtype),
            pltpu.VMEM((rows + 1, flow_rest.shape[1], steps, LANES), flow_rest.dtype),
            pltpu.SMEM((rows,), jnp.int32),
            pltpu.SMEM((blocks,), jnp.int32),
            pltpu.SMEM((blocks * (rows + UNROLL),), jnp.int32),
            pltpu.VMEM((size if leaving else TILE, LANES), jnp.float32),
            pltpu.SemaphoreType.DMA((steps // TILE, 2)),
            pltpu.SemaphoreType.DMA(()),
        ],
        compiler_params=params(58 if leaving else 50),
        name="leaving_sums" if leaving else "staying_sums",
    )(targets, density, flow_rest)


def merge_kernel(count, positions, size, messages, *refs):
    halves = len(positions)
    got, kept = refs[:messages], refs[messages:messages + halves]
    send, keeps, staged = refs[messages + halves], refs[messages + halves + 1:-1], refs[-1]
    half = count // 2
    largest = jnp.zeros((TILE, LANES), jnp.float32)
    for p in range(halves):
        message = got[min(p, messages - 1)]
        offset = (p if messages < halves else 0) * count * size
        factor = decode_factor(message[message.shape[0] - TILE:, :])

        def total(block, k):
            where = block * size + k * TILE
            return kept[p][rows_at(where), :] + decode(message[rows_at(offset + where), :], factor)

        def sent(i, top):
            def tile(k, top):
                piece = total(with_bit(i, positions[p], 1), k)
                staged[rows_at((p * half + i) * size + k * TILE), :] = piece
                return jnp.maximum(top, jnp.abs(piece))

            return lax.fori_loop(0, size // TILE, tile, top, unroll=4)

        largest = lax.fori_loop(0, half, sent, largest)

        def stay(i, carry):
            def tile(k, carry):
                keeps[p][rows_at(i * size + k * TILE), :] = total(with_bit(i, positions[p], 0), k)
                return carry

            return lax.fori_loop(0, size // TILE, tile, carry, unroll=4)

        lax.fori_loop(0, half, stay, 0)
    write_codes(largest, staged, send, halves * half * size)


def merge(got, kept, count, positions, size):
    rows = count // 2 * size
    halves = len(kept)
    made = pl.pallas_call(
        functools.partial(merge_kernel, count, tuple(positions), size, len(got)),
        out_shape=[jax.ShapeDtypeStruct((halves * rows + TILE, LANES), jnp.int16)]
        + [jax.ShapeDtypeStruct((rows, LANES), jnp.float32)] * halves,
        in_specs=[whole()] * (len(got) + halves),
        out_specs=[whole()] * (1 + halves),
        scratch_shapes=[pltpu.VMEM((halves * rows, LANES), jnp.float32)],
        compiler_params=params(),
        name="merge",
    )(*got, *kept)
    return made[0], list(made[1:])


def project(half, got_ref, kept_ref, proj_ref, weights_ref, totals):
    observers = weights_ref.shape[0]
    span = kept_ref.shape[0] // COMPS
    factor = decode_factor(got_ref[COMPS * span:COMPS * span + TILE, :])

    def fill(k, carry):
        where = rows_at(k * TILE)
        totals[where, :] = kept_ref[where, :] + decode(got_ref[where, :], factor)
        return carry

    lax.fori_loop(0, COMPS * span // TILE, fill, 0, unroll=4)
    lane = lax.broadcasted_iota(jnp.int32, (span, LANES), 1) % observers
    ones = jnp.ones((2 * LANES, LANES), jnp.bfloat16)
    at = slice(half * span, (half + 1) * span)
    parts = [totals[c * span:(c + 1) * span, :] for c in range(COMPS)]
    value = jnp.zeros((span, LANES), jnp.float32)
    for group in range(0, observers, GROUP):
        rows = []
        for o in range(group, group + GROUP):
            moment = proj_ref[o:o + 1, :] * parts[0]
            for c in range(1, COMPS):
                moment = moment + proj_ref[c * observers + o:c * observers + o + 1, :] * parts[c]
            term = weights_ref[o, at, :].astype(jnp.float32) * moment
            high = term.astype(jnp.bfloat16)
            low = (term - high.astype(jnp.float32)).astype(jnp.bfloat16)
            rows.append(jnp.concatenate([high, low], axis=1))
        sums = jnp.dot(jnp.concatenate(rows, axis=0), ones, preferred_element_type=jnp.float32)
        for u in range(GROUP):
            value = jnp.where(lane == group + u, sums[u * span:(u + 1) * span], value)
    return value


def first_kernel(proj_ref, got_ref, kept_ref, weights_ref, out_ref, totals):
    out_ref[...] = project(0, got_ref, kept_ref, proj_ref, weights_ref, totals)


def last_kernel(slabs, per_device, proj_ref, got_ref, kept_ref, weights_ref, first_ref, bins_ref, out_ref, totals):
    observers, steps, _ = weights_ref.shape
    source = jnp.concatenate(
        [first_ref[...], project(1, got_ref, kept_ref, proj_ref, weights_ref, totals)], axis=0
    )
    lead, period = 8, slabs * steps
    blank = jnp.zeros((lead, LANES), jnp.float32)
    value = jnp.concatenate([blank, source, blank], axis=0)
    size = value.shape[0]
    value = pltpu.roll(value, size - 1, 0) - 2.0 * value + pltpu.roll(value, 1, 0)
    value = jnp.concatenate([value, blank], axis=0)
    delay = bins_ref[...] + (lax.axis_index("tm") * steps + period - lead)
    delay = jnp.broadcast_to(jnp.where(delay >= period, delay - period, delay), (lead, LANES))
    delay = jnp.where(delay >= period, delay - period, delay)
    shift = 1
    while shift < lead:
        late = jnp.concatenate([(delay & shift) != 0] * (value.shape[0] // lead), axis=0)
        value = jnp.where(late, pltpu.roll(value, shift, 0), value)
        shift *= 2
    tiles = [value[k:k + lead] for k in range(0, value.shape[0], lead)]
    while shift < period // 2:
        far, late = shift // lead, (delay & shift) != 0
        padded = [blank] * far + tiles + [blank] * far
        tiles = [jnp.where(late, padded[k], padded[k + far]) for k in range(len(tiles) + far)]
        shift *= 2
    half = shift // lead
    tiles = tiles + [blank] * (2 * half - len(tiles))
    upper = lax.broadcasted_iota(jnp.int32, (lead, LANES), 1) >= observers
    late = ((delay & shift) != 0) != upper
    tiles = [jnp.where(late, tiles[k + half], tiles[k]) for k in range(half)]
    across = jnp.concatenate(tiles, axis=0).T
    rows = out_ref.shape[1]
    lane = lax.broadcasted_iota(jnp.int32, (per_device, LANES), 1)
    low = lane < steps
    for b in range(observers // per_device):
        for pair in range(period // LANES):
            first = pair * observers + b * per_device
            mine = across[first:first + per_device]
            turned = pltpu.roll(mine, steps, 1)
            if rows < per_device:
                down = jnp.concatenate([mine[rows:], mine[:rows]], axis=0)
                down_turned = jnp.concatenate([turned[rows:], turned[:rows]], axis=0)
                out_ref[b * slabs + 2 * pair] = jnp.where(low, mine, down_turned)[:rows]
                out_ref[b * slabs + 2 * pair + 1] = jnp.where(low, turned, down)[:rows]
            else:
                out_ref[b * slabs + 2 * pair] = mine
                out_ref[b * slabs + 2 * pair + 1] = turned


def sources(projector, got, kept, weights, bins, blocks, slabs):
    observers = weights.shape[0]
    per_device = observers // blocks
    rows = per_device // 2 if per_device % 2 == 0 else per_device
    size = kept[0].shape[0]
    first = pl.pallas_call(
        first_kernel,
        out_shape=jax.ShapeDtypeStruct((size // COMPS, LANES), jnp.float32),
        in_specs=[whole()] * 4,
        out_specs=whole(),
        scratch_shapes=[pltpu.VMEM((size, LANES), jnp.float32)],
        compiler_params=params(),
        name="first_sources",
    )(projector, got[0], kept[0], weights)
    return pl.pallas_call(
        functools.partial(last_kernel, slabs, per_device),
        out_shape=jax.ShapeDtypeStruct((blocks * slabs, rows, LANES), jnp.float32),
        in_specs=[whole()] * 6,
        out_specs=whole(),
        scratch_shapes=[pltpu.VMEM((size, LANES), jnp.float32)],
        compiler_params=params(),
        name="last_sources",
    )(projector, got[1], kept[1], weights, first, bins)


def record_kernel(got_ref, out_ref):
    per_device, steps = out_ref.shape
    total = got_ref[0]
    for k in range(1, got_ref.shape[0]):
        total = total + got_ref[k]
    rows = total.shape[0]
    out_ref[:rows, :] = total[:, :steps]
    if rows < per_device:
        out_ref[rows:, :] = total[:, steps:]


def records(got, per_device, steps):
    return pl.pallas_call(
        record_kernel,
        out_shape=jax.ShapeDtypeStruct((per_device, steps), jnp.float32),
        in_specs=[whole()],
        out_specs=whole(),
        compiler_params=params(),
        name="records",
    )(got)


def body(density, flow_rest, dest, weights, directions, bins):
    blocks, slabs = lax.axis_size("blk"), lax.axis_size("tm")
    steps = density.shape[1]
    observers = bins.shape[0]

    def swap(values, bit):
        return lax.ppermute(values, "blk", [(i, i ^ (1 << bit)) for i in range(blocks)])

    stages = blocks.bit_length() - 1
    orders = [list(range(stages)) for _ in range(2)]
    orders[1][:2] = [1, 0]
    size = COMPS * (steps // 2)
    bits = tuple(order[0] for order in orders)
    sends = stress_sums(density, flow_rest, dest[:, 0], blocks, bits, True)
    kept = stress_sums(density, flow_rest, dest[:, 0], blocks, bits, False)
    got = [swap(send, order[0]) for send, order in zip(sends, orders)]
    count = blocks // 2
    for stage in range(1, stages):
        places = [sorted(order[stage:]).index(order[stage]) for order in orders]
        made = [merge(got[p:p + 1], kept[p:p + 1], count, places[p:p + 1], size) for p in range(2)]
        got = [swap(made[p][0], orders[p][stage]) for p in range(2)]
        kept = made[0][1] + made[1][1]
        count //= 2

    d1, d2, d3 = [jnp.broadcast_to(directions[:, c:c + 1], (observers, LANES)) for c in range(3)]
    projector = jnp.concatenate(
        [d1 * d1, d2 * d2, d3 * d3, 2.0 * d1 * d2, 2.0 * d1 * d3, 2.0 * d2 * d3], axis=0
    )
    chunks = sources(projector, got, kept, weights[0], jnp.concatenate([bins.T] * 2, axis=1), blocks, slabs)
    chunks = lax.all_to_all(chunks, ("blk", "tm"), split_axis=0, concat_axis=0, tiled=True)
    return records(chunks, observers // blocks, steps)


def solution(mesh):
    placed = (
        P("blk", "tm", None),
        P("blk", None, "tm", None),
        P("blk", None),
        P("blk", None, "tm", None),
        P(),
        P(None, "blk"),
    )
    return jax.shard_map(
        body, mesh=mesh, in_specs=placed, out_specs=P("blk", "tm"), check_vma=False
    )
```

```python
import functools

import jax
import jax.numpy as jnp
from jax import lax
from jax.experimental import pallas as pl
from jax.experimental.pallas import tpu as pltpu
from jax.sharding import PartitionSpec as P

COMPS = 6
TILE = 16
LANES = 128
GROUP = 8
UNROLL = 4
GRAIN = 128.0
TOP = 32764.0
FLOOR = 1e-35


def whole():
    return pl.BlockSpec(memory_space=pltpu.VMEM)


def scalars():
    return pl.BlockSpec(memory_space=pltpu.SMEM)


def params(mebibytes=40):
    return pltpu.CompilerParams(vmem_limit_bytes=mebibytes * 1024 * 1024)


def scale_code(largest):
    return jnp.ceil(jnp.log(jnp.maximum(largest, FLOOR)) * GRAIN)


def encode(values, inverse):
    return jnp.round(values * inverse).astype(jnp.int32).astype(jnp.int16)


def encode_factor(code):
    return jnp.exp(code * (-1.0 / GRAIN)) * TOP


def decode_factor(code16):
    code = code16.astype(jnp.int32).astype(jnp.float32)
    return jnp.exp(code * (1.0 / GRAIN)) * (1.0 / TOP)


def decode(code16, factor):
    return code16.astype(jnp.int32).astype(jnp.float32) * factor


def with_bit(index, position, bit):
    low = index & ((1 << position) - 1)
    return ((index >> position) << (position + 1)) | (bit << position) | low


def rows_at(start, size=TILE):
    return pl.ds(pl.multiple_of(start, TILE), size)


def write_codes(largest, staged, send_ref, rows):
    code = scale_code(largest)
    inverse = encode_factor(code)

    def step(k, carry):
        where = rows_at(k * TILE)
        send_ref[where, :] = encode(staged[where, :], inverse)
        return carry

    lax.fori_loop(0, rows // TILE, step, 0, unroll=4)
    send_ref[rows:rows + TILE, :] = code.astype(jnp.int32).astype(jnp.int16)


def bucket(blocks, rows, dest_ref, counts, members):
    stride = rows + UNROLL

    def clear(b, carry):
        counts[b] = 0
        return carry

    lax.fori_loop(0, blocks, clear, 0)

    def place(r, carry):
        target = dest_ref[r]
        count = counts[target]
        members[target * stride + count] = r
        counts[target] = count + 1
        return carry

    lax.fori_loop(0, rows, place, 0, unroll=4)

    def pad(b, carry):
        end = b * stride + counts[b]
        for extra in range(UNROLL - 1):
            members[end + extra] = rows
        return carry

    lax.fori_loop(0, blocks, pad, 0)


def block_sums(target, at, stride, dens, flow, counts, members):
    first = target * stride

    def body(turn, totals):
        totals = list(totals)
        for u in range(UNROLL):
            row = members[first + turn * UNROLL + u]
            rho = dens[row, at, :].astype(jnp.float32)
            ux = flow[row, 0, at, :].astype(jnp.float32)
            uy = flow[row, 1, at, :].astype(jnp.float32)
            uz = flow[row, 2, at, :].astype(jnp.float32)
            excess = flow[row, 3, at, :].astype(jnp.float32)
            mx, my, mz = rho * ux, rho * uy, rho * uz
            for i, term in enumerate((mx * ux, my * uy, mz * uz, mx * uy, mx * uz, my * uz, excess)):
                totals[i] = totals[i] + term
        return tuple(totals)

    zero = jnp.zeros((TILE, LANES), jnp.float32)
    turns = (counts[target] + (UNROLL - 1)) // UNROLL
    xx, yy, zz, xy, xz, yz, excess = lax.fori_loop(0, turns, body, (zero,) * 7)
    return xx + excess, yy + excess, zz + excess, xy, xz, yz


def leaving_kernel(blocks, halves, dest_ref, density_ref, flow_ref, *refs):
    sends, (dens, flow, counts, members) = refs[:halves], refs[halves:halves + 4]
    dest, staged, sems, dest_sem = refs[halves + 4:]
    rows, steps = density_ref.shape[0], density_ref.shape[1]
    per_half = steps // TILE // halves
    span = steps // halves
    fetch = pltpu.make_async_copy(dest_ref, dest, dest_sem)
    fetch.start()
    copies = []
    for k in range(steps // TILE):
        at = pl.ds(k * TILE, TILE)
        pair = (
            pltpu.make_async_copy(density_ref.at[:, at, :], dens.at[pl.ds(0, rows), at, :], sems.at[k, 0]),
            pltpu.make_async_copy(flow_ref.at[:, :, at, :], flow.at[pl.ds(0, rows), :, at, :], sems.at[k, 1]),
        )
        for copy in pair:
            copy.start()
        copies.append(pair)

    dens[rows] = jnp.zeros_like(dens[rows])
    flow[rows] = jnp.zeros_like(flow[rows])
    fetch.wait()
    bucket(blocks, rows, dest, counts, members)
    for half in range(halves):
        largest = jnp.zeros((TILE, LANES), jnp.float32)
        for k in range(per_half):
            tile = half * per_half + k
            for copy in copies[tile]:
                copy.wait()

            def block(i, top):
                pieces = slot_sums(half, i, 1, tile, dens, flow, counts, members)
                for c, piece in enumerate(pieces):
                    staged[rows_at((i * COMPS + c) * span + k * TILE), :] = piece
                    top = jnp.maximum(top, jnp.abs(piece))
                return top

            largest = lax.fori_loop(0, blocks // 2, block, largest)
        write_codes(largest, staged, sends[half], blocks // 2 * COMPS * span)


def staying_kernel(blocks, halves, dens, flow, counts, members, *outs):
    steps = dens.shape[1]
    per_half = steps // TILE // halves
    span = steps // halves
    for half in range(halves):
        for k in range(per_half):
            def block(i, carry):
                pieces = slot_sums(half, i, 0, half * per_half + k, dens, flow, counts, members)
                for c, piece in enumerate(pieces):
                    outs[half][rows_at((i * COMPS + c) * span + k * TILE), :] = piece
                return carry

            lax.fori_loop(0, blocks // 2, block, 0)


def slot_sums(half, slot, leaving, tile, dens, flow, counts, members):
    bit = half
    target = lax.axis_index("blk") ^ with_bit(slot, bit, leaving)
    at = slice(tile * TILE, (tile + 1) * TILE)
    return block_sums(target, at, dens.shape[0] - 1 + UNROLL, dens, flow, counts, members)


def leaving_sums(density, flow_rest, targets, blocks, halves):
    rows, steps, _ = density.shape
    size = blocks // 2 * COMPS * (steps // halves)
    made = pl.pallas_call(
        functools.partial(leaving_kernel, blocks, halves),
        out_shape=[pltpu.VMEM((size + TILE, LANES), jnp.int16)] * halves + [
            pltpu.VMEM((rows + 1, steps, LANES), density.dtype),
            pltpu.VMEM((rows + 1, flow_rest.shape[1], steps, LANES), flow_rest.dtype),
            pltpu.SMEM((blocks,), jnp.int32),
            pltpu.SMEM((blocks * (rows + UNROLL),), jnp.int32),
        ],
        in_specs=[pl.BlockSpec(memory_space=pltpu.HBM)] * 3,
        out_specs=[whole()] * (halves + 2) + [scalars()] * 2,
        scratch_shapes=[
            pltpu.SMEM((rows,), jnp.int32),
            pltpu.VMEM((size, LANES), jnp.float32),
            pltpu.SemaphoreType.DMA((steps // TILE, 2)),
            pltpu.SemaphoreType.DMA(()),
        ],
        compiler_params=params(24),
        name="leaving_sums",
    )(pltpu.with_memory_space_constraint(targets, pltpu.HBM), pltpu.with_memory_space_constraint(density, pltpu.HBM), pltpu.with_memory_space_constraint(flow_rest, pltpu.HBM))
    return list(made[:halves]), list(made[halves:])


def staying_sums(held, blocks, halves):
    size = blocks // 2 * COMPS * (held[0].shape[1] // halves)
    return pl.pallas_call(
        functools.partial(staying_kernel, blocks, halves),
        out_shape=[jax.ShapeDtypeStruct((size, LANES), jnp.float32)] * halves,
        in_specs=[whole()] * 2 + [scalars()] * 2,
        out_specs=[whole()] * halves,
        compiler_params=params(16),
        name="staying_sums",
    )(*held)


def merge_kernel(count, positions, size, messages, *refs):
    halves = len(positions)
    got, kept = refs[:messages], refs[messages:messages + halves]
    send, keeps, staged = refs[messages + halves], refs[messages + halves + 1:-1], refs[-1]
    half = count // 2
    largest = jnp.zeros((TILE, LANES), jnp.float32)
    for p in range(halves):
        message = got[min(p, messages - 1)]
        offset = (p if messages < halves else 0) * count * size
        factor = decode_factor(message[message.shape[0] - TILE:, :])

        def total(block, k):
            where = block * size + k * TILE
            return kept[p][rows_at(where), :] + decode(message[rows_at(offset + where), :], factor)

        def sent(i, top):
            def tile(k, top):
                piece = total(with_bit(i, positions[p], 1), k)
                staged[rows_at((p * half + i) * size + k * TILE), :] = piece
                return jnp.maximum(top, jnp.abs(piece))

            return lax.fori_loop(0, size // TILE, tile, top, unroll=4)

        largest = lax.fori_loop(0, half, sent, largest)

        def stay(i, carry):
            def tile(k, carry):
                keeps[p][rows_at(i * size + k * TILE), :] = total(with_bit(i, positions[p], 0), k)
                return carry

            return lax.fori_loop(0, size // TILE, tile, carry, unroll=4)

        lax.fori_loop(0, half, stay, 0)
    write_codes(largest, staged, send, halves * half * size)


def merge(got, kept, count, positions, size):
    rows = count // 2 * size
    halves = len(kept)
    made = pl.pallas_call(
        functools.partial(merge_kernel, count, tuple(positions), size, len(got)),
        out_shape=[jax.ShapeDtypeStruct((halves * rows + TILE, LANES), jnp.int16)]
        + [jax.ShapeDtypeStruct((rows, LANES), jnp.float32)] * halves,
        in_specs=[whole()] * (len(got) + halves),
        out_specs=[whole()] * (1 + halves),
        scratch_shapes=[pltpu.VMEM((halves * rows, LANES), jnp.float32)],
        compiler_params=params(),
        name="merge",
    )(*got, *kept)
    return made[0], list(made[1:])


def project(half, got_ref, kept_ref, proj_ref, weights_ref, totals):
    observers = weights_ref.shape[0]
    span = kept_ref.shape[0] // COMPS
    factor = decode_factor(got_ref[COMPS * span:COMPS * span + TILE, :])

    def fill(k, carry):
        where = rows_at(k * TILE)
        totals[where, :] = kept_ref[where, :] + decode(got_ref[where, :], factor)
        return carry

    lax.fori_loop(0, COMPS * span // TILE, fill, 0, unroll=4)
    lane = lax.broadcasted_iota(jnp.int32, (span, LANES), 1) % observers
    ones = jnp.ones((2 * LANES, LANES), jnp.bfloat16)
    at = slice(half * span, (half + 1) * span)
    parts = [totals[c * span:(c + 1) * span, :] for c in range(COMPS)]
    value = jnp.zeros((span, LANES), jnp.float32)
    for group in range(0, observers, GROUP):
        rows = []
        for o in range(group, group + GROUP):
            moment = proj_ref[o:o + 1, :] * parts[0]
            for c in range(1, COMPS):
                moment = moment + proj_ref[c * observers + o:c * observers + o + 1, :] * parts[c]
            term = weights_ref[o, at, :].astype(jnp.float32) * moment
            high = term.astype(jnp.bfloat16)
            low = (term - high.astype(jnp.float32)).astype(jnp.bfloat16)
            rows.append(jnp.concatenate([high, low], axis=1))
        sums = jnp.dot(jnp.concatenate(rows, axis=0), ones, preferred_element_type=jnp.float32)
        for u in range(GROUP):
            value = jnp.where(lane == group + u, sums[u * span:(u + 1) * span], value)
    return value


def first_kernel(proj_ref, got_ref, kept_ref, weights_ref, out_ref, totals):
    out_ref[...] = project(0, got_ref, kept_ref, proj_ref, weights_ref, totals)


def last_kernel(slabs, per_device, proj_ref, got_ref, kept_ref, weights_ref, first_ref, bins_ref, out_ref, totals):
    observers, steps, _ = weights_ref.shape
    source = jnp.concatenate(
        [first_ref[...], project(1, got_ref, kept_ref, proj_ref, weights_ref, totals)], axis=0
    )
    lead, period = 8, slabs * steps
    blank = jnp.zeros((lead, LANES), jnp.float32)
    value = jnp.concatenate([blank, source, blank], axis=0)
    size = value.shape[0]
    value = pltpu.roll(value, size - 1, 0) - 2.0 * value + pltpu.roll(value, 1, 0)
    value = jnp.concatenate([value, blank], axis=0)
    delay = bins_ref[...] + (lax.axis_index("tm") * steps + period - lead)
    delay = jnp.broadcast_to(jnp.where(delay >= period, delay - period, delay), (lead, LANES))
    delay = jnp.where(delay >= period, delay - period, delay)
    shift = 1
    while shift < lead:
        late = jnp.concatenate([(delay & shift) != 0] * (value.shape[0] // lead), axis=0)
        value = jnp.where(late, pltpu.roll(value, shift, 0), value)
        shift *= 2
    tiles = [value[k:k + lead] for k in range(0, value.shape[0], lead)]
    while shift < period // 2:
        far, late = shift // lead, (delay & shift) != 0
        padded = [blank] * far + tiles + [blank] * far
        tiles = [jnp.where(late, padded[k], padded[k + far]) for k in range(len(tiles) + far)]
        shift *= 2
    half = shift // lead
    tiles = tiles + [blank] * (2 * half - len(tiles))
    upper = lax.broadcasted_iota(jnp.int32, (lead, LANES), 1) >= observers
    late = ((delay & shift) != 0) != upper
    tiles = [jnp.where(late, tiles[k + half], tiles[k]) for k in range(half)]
    across = jnp.concatenate(tiles, axis=0).T
    rows = out_ref.shape[1]
    lane = lax.broadcasted_iota(jnp.int32, (per_device, LANES), 1)
    low = lane < steps
    for b in range(observers // per_device):
        for pair in range(period // LANES):
            first = pair * observers + b * per_device
            mine = across[first:first + per_device]
            turned = pltpu.roll(mine, steps, 1)
            if rows < per_device:
                down = jnp.concatenate([mine[rows:], mine[:rows]], axis=0)
                down_turned = jnp.concatenate([turned[rows:], turned[:rows]], axis=0)
                out_ref[b * slabs + 2 * pair] = jnp.where(low, mine, down_turned)[:rows]
                out_ref[b * slabs + 2 * pair + 1] = jnp.where(low, turned, down)[:rows]
            else:
                out_ref[b * slabs + 2 * pair] = mine
                out_ref[b * slabs + 2 * pair + 1] = turned


def sources(projector, got, kept, weights, bins, blocks, slabs):
    observers = weights.shape[0]
    per_device = observers // blocks
    rows = per_device // 2 if per_device % 2 == 0 else per_device
    size = kept[0].shape[0]
    first = pl.pallas_call(
        first_kernel,
        out_shape=jax.ShapeDtypeStruct((size // COMPS, LANES), jnp.float32),
        in_specs=[whole()] * 4,
        out_specs=whole(),
        scratch_shapes=[pltpu.VMEM((size, LANES), jnp.float32)],
        compiler_params=params(),
        name="first_sources",
    )(projector, got[0], kept[0], weights)
    return pl.pallas_call(
        functools.partial(last_kernel, slabs, per_device),
        out_shape=jax.ShapeDtypeStruct((blocks * slabs, rows, LANES), jnp.float32),
        in_specs=[whole()] * 6,
        out_specs=whole(),
        scratch_shapes=[pltpu.VMEM((size, LANES), jnp.float32)],
        compiler_params=params(),
        name="last_sources",
    )(projector, got[1], kept[1], weights, first, bins)


def record_kernel(got_ref, out_ref):
    per_device, steps = out_ref.shape
    total = got_ref[0]
    for k in range(1, got_ref.shape[0]):
        total = total + got_ref[k]
    rows = total.shape[0]
    out_ref[:rows, :] = total[:, :steps]
    if rows < per_device:
        out_ref[rows:, :] = total[:, steps:]


def records(got, per_device, steps):
    return pl.pallas_call(
        record_kernel,
        out_shape=jax.ShapeDtypeStruct((per_device, steps), jnp.float32),
        in_specs=[whole()],
        out_specs=whole(),
        compiler_params=params(),
        name="records",
    )(got)


def body(density, flow_rest, dest, weights, directions, bins):
    blocks, slabs = lax.axis_size("blk"), lax.axis_size("tm")
    steps = density.shape[1]
    observers = bins.shape[0]

    def swap(values, bit):
        return lax.ppermute(values, "blk", [(i, i ^ (1 << bit)) for i in range(blocks)])

    stages = blocks.bit_length() - 1
    orders = [list(range(stages)) for _ in range(2)]
    orders[1][:2] = [1, 0]
    size = COMPS * (steps // 2)
    bits = tuple(order[0] for order in orders)
    sends, held = leaving_sums(density, flow_rest, dest[:, 0], blocks, 2)
    kept = staying_sums(held, blocks, 2)
    got = [swap(send, order[0]) for send, order in zip(sends, orders)]
    count = blocks // 2
    for stage in range(1, stages):
        places = [sorted(order[stage:]).index(order[stage]) for order in orders]
        made = [merge(got[p:p + 1], kept[p:p + 1], count, places[p:p + 1], size) for p in range(2)]
        got = [swap(made[p][0], orders[p][stage]) for p in range(2)]
        kept = made[0][1] + made[1][1]
        count //= 2

    d1, d2, d3 = [jnp.broadcast_to(directions[:, c:c + 1], (observers, LANES)) for c in range(3)]
    projector = jnp.concatenate(
        [d1 * d1, d2 * d2, d3 * d3, 2.0 * d1 * d2, 2.0 * d1 * d3, 2.0 * d2 * d3], axis=0
    )
    chunks = sources(projector, got, kept, weights[0], jnp.concatenate([bins.T] * 2, axis=1), blocks, slabs)
    chunks = lax.all_to_all(chunks, ("blk", "tm"), split_axis=0, concat_axis=0, tiled=True)
    return records(chunks, observers // blocks, steps)


def solution(mesh):
    placed = (
        P("blk", "tm", None),
        P("blk", None, "tm", None),
        P("blk", None),
        P("blk", None, "tm", None),
        P(),
        P(None, "blk"),
    )
    return jax.shard_map(
        body, mesh=mesh, in_specs=placed, out_specs=P("blk", "tm"), check_vma=False
    )
```

```python
import functools

import jax
import jax.numpy as jnp
from jax import lax
from jax.experimental import pallas as pl
from jax.experimental.pallas import tpu as pltpu
from jax.sharding import PartitionSpec as P

COMPS = 6
TILE = 16
LANES = 128
GROUP = 8
UNROLL = 4
GRAIN = 128.0
TOP = 32764.0
FLOOR = 1e-33


def whole():
    return pl.BlockSpec(memory_space=pltpu.VMEM)


def scalars():
    return pl.BlockSpec(memory_space=pltpu.SMEM)


def params(mebibytes=40):
    return pltpu.CompilerParams(vmem_limit_bytes=mebibytes * 1024 * 1024)


def scale_code(largest):
    return jnp.ceil(jnp.log(jnp.maximum(largest, FLOOR)) * GRAIN)


def encode(values, inverse):
    return jnp.round(values * inverse).astype(jnp.int32).astype(jnp.int16)


def encode_factor(code):
    return jnp.exp(code * (-1.0 / GRAIN)) * TOP


def decode_factor(code16):
    code = code16.astype(jnp.int32).astype(jnp.float32)
    return jnp.exp(code * (1.0 / GRAIN)) * (1.0 / TOP)


def decode(code16, factor):
    return code16.astype(jnp.int32).astype(jnp.float32) * factor


def with_bit(index, position, bit):
    low = index & ((1 << position) - 1)
    return ((index >> position) << (position + 1)) | (bit << position) | low


def rows_at(start, size=TILE):
    return pl.ds(pl.multiple_of(start, TILE), size)


def write_codes(largest, staged, send_ref, rows):
    code = scale_code(largest)
    inverse = encode_factor(code)

    def step(k, carry):
        where = rows_at(k * TILE)
        send_ref[where, :] = encode(staged[where, :], inverse)
        return carry

    lax.fori_loop(0, rows // TILE, step, 0, unroll=4)
    send_ref[rows:rows + TILE, :] = code.astype(jnp.int32).astype(jnp.int16)


def bucket(blocks, rows, dest_ref, counts, members):
    stride = rows + UNROLL

    def clear(b, carry):
        counts[b] = 0
        return carry

    lax.fori_loop(0, blocks, clear, 0)

    def place(r, carry):
        target = dest_ref[r]
        count = counts[target]
        members[target * stride + count] = r
        counts[target] = count + 1
        return carry

    lax.fori_loop(0, rows, place, 0, unroll=4)

    def pad(b, carry):
        end = b * stride + counts[b]
        for extra in range(UNROLL - 1):
            members[end + extra] = rows
        return carry

    lax.fori_loop(0, blocks, pad, 0)


def block_sums(target, at, stride, dens, flow, counts, members):
    first = target * stride

    def body(turn, totals):
        totals = list(totals)
        for u in range(UNROLL):
            row = members[first + turn * UNROLL + u]
            rho = dens[row, at, :].astype(jnp.float32)
            ux = flow[row, 0, at, :].astype(jnp.float32)
            uy = flow[row, 1, at, :].astype(jnp.float32)
            uz = flow[row, 2, at, :].astype(jnp.float32)
            excess = flow[row, 3, at, :].astype(jnp.float32)
            mx, my, mz = rho * ux, rho * uy, rho * uz
            for i, term in enumerate((mx * ux, my * uy, mz * uz, mx * uy, mx * uz, my * uz, excess)):
                totals[i] = totals[i] + term
        return tuple(totals)

    zero = jnp.zeros((TILE, LANES), jnp.float32)
    turns = (counts[target] + (UNROLL - 1)) // UNROLL
    xx, yy, zz, xy, xz, yz, excess = lax.fori_loop(0, turns, body, (zero,) * 7)
    return xx + excess, yy + excess, zz + excess, xy, xz, yz


def leaving_kernel(blocks, halves, dest_ref, density_ref, flow_ref, *refs):
    sends, (dens, flow, counts, members) = refs[:halves], refs[halves:halves + 4]
    dest, staged, sems, dest_sem = refs[halves + 4:]
    rows, steps = density_ref.shape[0], density_ref.shape[1]
    per_half = steps // TILE // halves
    span = steps // halves
    fetch = pltpu.make_async_copy(dest_ref, dest, dest_sem)
    fetch.start()
    copies = []
    for k in range(steps // TILE):
        at = pl.ds(k * TILE, TILE)
        pair = (
            pltpu.make_async_copy(density_ref.at[:, at, :], dens.at[pl.ds(0, rows), at, :], sems.at[k, 0]),
            pltpu.make_async_copy(flow_ref.at[:, :, at, :], flow.at[pl.ds(0, rows), :, at, :], sems.at[k, 1]),
        )
        for copy in pair:
            copy.start()
        copies.append(pair)

    dens[rows] = jnp.zeros_like(dens[rows])
    flow[rows] = jnp.zeros_like(flow[rows])
    fetch.wait()
    bucket(blocks, rows, dest, counts, members)
    for half in range(halves):
        largest = jnp.zeros((TILE, LANES), jnp.float32)
        for k in range(per_half):
            tile = half * per_half + k
            for copy in copies[tile]:
                copy.wait()

            def block(i, top):
                pieces = slot_sums(half, i, 1, tile, dens, flow, counts, members)
                for c, piece in enumerate(pieces):
                    staged[rows_at((i * COMPS + c) * span + k * TILE), :] = piece
                    top = jnp.maximum(top, jnp.abs(piece))
                return top

            largest = lax.fori_loop(0, blocks // 2, block, largest)
        write_codes(largest, staged, sends[half], blocks // 2 * COMPS * span)


def staying_kernel(blocks, halves, dens, flow, counts, members, *outs):
    steps = dens.shape[1]
    per_half = steps // TILE // halves
    span = steps // halves
    for half in range(halves):
        for k in range(per_half):
            def block(i, carry):
                pieces = slot_sums(half, i, 0, half * per_half + k, dens, flow, counts, members)
                for c, piece in enumerate(pieces):
                    outs[half][rows_at((i * COMPS + c) * span + k * TILE), :] = piece
                return carry

            lax.fori_loop(0, blocks // 2, block, 0)


def slot_sums(half, slot, leaving, tile, dens, flow, counts, members):
    bit = half
    target = lax.axis_index("blk") ^ with_bit(slot, bit, leaving)
    at = slice(tile * TILE, (tile + 1) * TILE)
    return block_sums(target, at, dens.shape[0] - 1 + UNROLL, dens, flow, counts, members)


def leaving_sums(density, flow_rest, targets, blocks, halves):
    rows, steps, _ = density.shape
    size = blocks // 2 * COMPS * (steps // halves)
    made = pl.pallas_call(
        functools.partial(leaving_kernel, blocks, halves),
        out_shape=[pltpu.VMEM((size + TILE, LANES), jnp.int16)] * halves + [
            pltpu.VMEM((rows + 1, steps, LANES), density.dtype),
            pltpu.VMEM((rows + 1, flow_rest.shape[1], steps, LANES), flow_rest.dtype),
            pltpu.SMEM((blocks,), jnp.int32),
            pltpu.SMEM((blocks * (rows + UNROLL),), jnp.int32),
        ],
        in_specs=[pl.BlockSpec(memory_space=pltpu.HBM)] * 3,
        out_specs=[whole()] * (halves + 2) + [scalars()] * 2,
        scratch_shapes=[
            pltpu.SMEM((rows,), jnp.int32),
            pltpu.VMEM((size, LANES), jnp.float32),
            pltpu.SemaphoreType.DMA((steps // TILE, 2)),
            pltpu.SemaphoreType.DMA(()),
        ],
        compiler_params=params(24),
        name="leaving_sums",
    )(pltpu.with_memory_space_constraint(targets, pltpu.HBM), pltpu.with_memory_space_constraint(density, pltpu.HBM), pltpu.with_memory_space_constraint(flow_rest, pltpu.HBM))
    return list(made[:halves]), list(made[halves:])


def staying_sums(held, blocks, halves):
    size = blocks // 2 * COMPS * (held[0].shape[1] // halves)
    return pl.pallas_call(
        functools.partial(staying_kernel, blocks, halves),
        out_shape=[jax.ShapeDtypeStruct((size, LANES), jnp.float32)] * halves,
        in_specs=[whole()] * 2 + [scalars()] * 2,
        out_specs=[whole()] * halves,
        compiler_params=params(16),
        name="staying_sums",
    )(*held)


def total_at(got, kept, factor, where):
    return kept[rows_at(where), :] + decode(got[rows_at(where), :], factor)


def send_kernel(count, position, size, got, kept, send, staged):
    factor = decode_factor(got[count * size:count * size + TILE, :])

    def block(i, top):
        def tile(k, top):
            piece = total_at(got, kept, factor, with_bit(i, position, 1) * size + k * TILE)
            staged[rows_at(i * size + k * TILE), :] = piece
            return jnp.maximum(top, jnp.abs(piece))

        return lax.fori_loop(0, size // TILE, tile, top, unroll=4)

    largest = lax.fori_loop(0, count // 2, block, jnp.zeros((TILE, LANES), jnp.float32))
    write_codes(largest, staged, send, count // 2 * size)


def keep_kernel(count, position, size, got, kept, keep):
    factor = decode_factor(got[count * size:count * size + TILE, :])

    def block(i, carry):
        def tile(k, carry):
            keep[rows_at(i * size + k * TILE), :] = total_at(got, kept, factor, with_bit(i, position, 0) * size + k * TILE)
            return carry

        return lax.fori_loop(0, size // TILE, tile, carry, unroll=4)

    lax.fori_loop(0, count // 2, block, 0)


def merge(got, kept, count, position, size):
    rows = count // 2 * size
    send = pl.pallas_call(
        functools.partial(send_kernel, count, position, size),
        out_shape=jax.ShapeDtypeStruct((rows + TILE, LANES), jnp.int16),
        in_specs=[whole()] * 2,
        out_specs=whole(),
        scratch_shapes=[pltpu.VMEM((rows, LANES), jnp.float32)],
        compiler_params=params(),
        name="merge_sent",
    )(got, kept)
    keep = pl.pallas_call(
        functools.partial(keep_kernel, count, position, size),
        out_shape=jax.ShapeDtypeStruct((rows, LANES), jnp.float32),
        in_specs=[whole()] * 2,
        out_specs=whole(),
        compiler_params=params(),
        name="merge_kept",
    )(got, kept)
    return send, keep


def project(half, got_ref, kept_ref, proj_ref, weights_ref, totals):
    observers = weights_ref.shape[0]
    span = kept_ref.shape[0] // COMPS
    factor = decode_factor(got_ref[COMPS * span:COMPS * span + TILE, :])

    def fill(k, carry):
        where = rows_at(k * TILE)
        totals[where, :] = kept_ref[where, :] + decode(got_ref[where, :], factor)
        return carry

    lax.fori_loop(0, COMPS * span // TILE, fill, 0, unroll=4)
    lane = lax.broadcasted_iota(jnp.int32, (span, LANES), 1) % observers
    ones = jnp.ones((2 * LANES, LANES), jnp.bfloat16)
    at = slice(half * span, (half + 1) * span)
    parts = [totals[c * span:(c + 1) * span, :] for c in range(COMPS)]
    value = jnp.zeros((span, LANES), jnp.float32)
    for group in range(0, observers, GROUP):
        rows = []
        for o in range(group, group + GROUP):
            moment = proj_ref[o:o + 1, :] * parts[0]
            for c in range(1, COMPS):
                moment = moment + proj_ref[c * observers + o:c * observers + o + 1, :] * parts[c]
            term = weights_ref[o, at, :].astype(jnp.float32) * moment
            high = term.astype(jnp.bfloat16)
            low = (term - high.astype(jnp.float32)).astype(jnp.bfloat16)
            rows.append(jnp.concatenate([high, low], axis=1))
        sums = jnp.dot(jnp.concatenate(rows, axis=0), ones, preferred_element_type=jnp.float32)
        for u in range(GROUP):
            value = jnp.where(lane == group + u, sums[u * span:(u + 1) * span], value)
    return value


def first_kernel(proj_ref, got_ref, kept_ref, weights_ref, out_ref, totals):
    out_ref[...] = project(0, got_ref, kept_ref, proj_ref, weights_ref, totals)


def last_kernel(slabs, per_device, proj_ref, got_ref, kept_ref, weights_ref, first_ref, bins_ref, out_ref, totals):
    observers, steps, _ = weights_ref.shape
    source = jnp.concatenate(
        [first_ref[...], project(1, got_ref, kept_ref, proj_ref, weights_ref, totals)], axis=0
    )
    lead, period = 8, slabs * steps
    blank = jnp.zeros((lead, LANES), jnp.float32)
    value = jnp.concatenate([blank, source, blank], axis=0)
    size = value.shape[0]
    value = pltpu.roll(value, size - 1, 0) - 2.0 * value + pltpu.roll(value, 1, 0)
    value = jnp.concatenate([value, blank], axis=0)
    delay = bins_ref[...] + (lax.axis_index("tm") * steps + period - lead)
    delay = jnp.broadcast_to(jnp.where(delay >= period, delay - period, delay), (lead, LANES))
    delay = jnp.where(delay >= period, delay - period, delay)
    shift = 1
    while shift < lead:
        late = jnp.concatenate([(delay & shift) != 0] * (value.shape[0] // lead), axis=0)
        value = jnp.where(late, pltpu.roll(value, shift, 0), value)
        shift *= 2
    tiles = [value[k:k + lead] for k in range(0, value.shape[0], lead)]
    while shift < period // 2:
        far, late = shift // lead, (delay & shift) != 0
        padded = [blank] * far + tiles + [blank] * far
        tiles = [jnp.where(late, padded[k], padded[k + far]) for k in range(len(tiles) + far)]
        shift *= 2
    half = shift // lead
    tiles = tiles + [blank] * (2 * half - len(tiles))
    upper = lax.broadcasted_iota(jnp.int32, (lead, LANES), 1) >= observers
    late = ((delay & shift) != 0) != upper
    tiles = [jnp.where(late, tiles[k + half], tiles[k]) for k in range(half)]
    across = jnp.concatenate(tiles, axis=0).T
    rows = out_ref.shape[1]
    lane = lax.broadcasted_iota(jnp.int32, (per_device, LANES), 1)
    low = lane < steps
    for b in range(observers // per_device):
        for pair in range(period // LANES):
            first = pair * observers + b * per_device
            mine = across[first:first + per_device]
            turned = pltpu.roll(mine, steps, 1)
            if rows < per_device:
                down = jnp.concatenate([mine[rows:], mine[:rows]], axis=0)
                down_turned = jnp.concatenate([turned[rows:], turned[:rows]], axis=0)
                out_ref[b * slabs + 2 * pair] = jnp.where(low, mine, down_turned)[:rows]
                out_ref[b * slabs + 2 * pair + 1] = jnp.where(low, turned, down)[:rows]
            else:
                out_ref[b * slabs + 2 * pair] = mine
                out_ref[b * slabs + 2 * pair + 1] = turned


def sources(projector, got, kept, weights, bins, blocks, slabs):
    observers = weights.shape[0]
    per_device = observers // blocks
    rows = per_device // 2 if per_device % 2 == 0 else per_device
    size = kept[0].shape[0]
    first = pl.pallas_call(
        first_kernel,
        out_shape=jax.ShapeDtypeStruct((size // COMPS, LANES), jnp.float32),
        in_specs=[whole()] * 4,
        out_specs=whole(),
        scratch_shapes=[pltpu.VMEM((size, LANES), jnp.float32)],
        compiler_params=params(),
        name="first_sources",
    )(projector, got[0], kept[0], weights)
    return pl.pallas_call(
        functools.partial(last_kernel, slabs, per_device),
        out_shape=jax.ShapeDtypeStruct((blocks * slabs, rows, LANES), jnp.float32),
        in_specs=[whole()] * 6,
        out_specs=whole(),
        scratch_shapes=[pltpu.VMEM((size, LANES), jnp.float32)],
        compiler_params=params(),
        name="last_sources",
    )(projector, got[1], kept[1], weights, first, bins)


def record_kernel(got_ref, out_ref):
    per_device, steps = out_ref.shape
    total = got_ref[0]
    for k in range(1, got_ref.shape[0]):
        total = total + got_ref[k]
    rows = total.shape[0]
    out_ref[:rows, :] = total[:, :steps]
    if rows < per_device:
        out_ref[rows:, :] = total[:, steps:]


def records(got, per_device, steps):
    return pl.pallas_call(
        record_kernel,
        out_shape=jax.ShapeDtypeStruct((per_device, steps), jnp.float32),
        in_specs=[whole()],
        out_specs=whole(),
        compiler_params=params(),
        name="records",
    )(got)


def body(density, flow_rest, dest, weights, directions, bins):
    blocks, slabs = lax.axis_size("blk"), lax.axis_size("tm")
    steps = density.shape[1]
    observers = bins.shape[0]

    def swap(values, bit):
        return lax.ppermute(values, "blk", [(i, i ^ (1 << bit)) for i in range(blocks)])

    stages = blocks.bit_length() - 1
    orders = [list(range(stages)) for _ in range(2)]
    orders[1][:2] = [1, 0]
    size = COMPS * (steps // 2)
    bits = tuple(order[0] for order in orders)
    sends, held = leaving_sums(density, flow_rest, dest[:, 0], blocks, 2)
    kept = staying_sums(held, blocks, 2)
    got = [swap(send, order[0]) for send, order in zip(sends, orders)]
    count = blocks // 2
    for stage in range(1, stages):
        places = [sorted(order[stage:]).index(order[stage]) for order in orders]
        made = [merge(got[p], kept[p], count, places[p], size) for p in range(2)]
        got = [swap(made[p][0], orders[p][stage]) for p in range(2)]
        kept = [made[p][1] for p in range(2)]
        count //= 2

    d1, d2, d3 = [jnp.broadcast_to(directions[:, c:c + 1], (observers, LANES)) for c in range(3)]
    projector = jnp.concatenate(
        [d1 * d1, d2 * d2, d3 * d3, 2.0 * d1 * d2, 2.0 * d1 * d3, 2.0 * d2 * d3], axis=0
    )
    chunks = sources(projector, got, kept, weights[0], jnp.concatenate([bins.T] * 2, axis=1), blocks, slabs)
    chunks = lax.all_to_all(chunks, ("blk", "tm"), split_axis=0, concat_axis=0, tiled=True)
    return records(chunks, observers // blocks, steps)


def solution(mesh):
    placed = (
        P("blk", "tm", None),
        P("blk", None, "tm", None),
        P("blk", None),
        P("blk", None, "tm", None),
        P(),
        P(None, "blk"),
    )
    return jax.shard_map(
        body, mesh=mesh, in_specs=placed, out_specs=P("blk", "tm"), check_vma=False
    )
```

```python
import functools

import jax
import jax.numpy as jnp
from jax import lax
from jax.experimental import pallas as pl
from jax.experimental.pallas import tpu as pltpu
from jax.sharding import PartitionSpec as P

COMPS = 6
TILE = 16
LANES = 128
GROUP = 8
UNROLL = 4
GRAIN = 128.0
TOP = 32764.0
FLOOR = 1e-33


def whole():
    return pl.BlockSpec(memory_space=pltpu.VMEM)


def scalars():
    return pl.BlockSpec(memory_space=pltpu.SMEM)


def params(mebibytes=40):
    return pltpu.CompilerParams(vmem_limit_bytes=mebibytes * 1024 * 1024)


def scale_code(largest):
    return jnp.ceil(jnp.log(jnp.maximum(largest, FLOOR)) * GRAIN)


def encode(values, inverse):
    return jnp.round(values * inverse).astype(jnp.int32).astype(jnp.int16)


def encode_factor(code):
    return jnp.exp(code * (-1.0 / GRAIN)) * TOP


def decode_factor(code16):
    code = code16.astype(jnp.int32).astype(jnp.float32)
    return jnp.exp(code * (1.0 / GRAIN)) * (1.0 / TOP)


def decode(code16, factor):
    return code16.astype(jnp.int32).astype(jnp.float32) * factor


def with_bit(index, position, bit):
    low = index & ((1 << position) - 1)
    return ((index >> position) << (position + 1)) | (bit << position) | low


def rows_at(start, size=TILE):
    return pl.ds(pl.multiple_of(start, TILE), size)


def write_codes(largest, staged, send_ref, rows):
    code = scale_code(largest)
    inverse = encode_factor(code)

    def step(k, carry):
        where = rows_at(k * TILE)
        send_ref[where, :] = encode(staged[where, :], inverse)
        return carry

    lax.fori_loop(0, rows // TILE, step, 0, unroll=8)
    send_ref[rows:rows + TILE, :] = code.astype(jnp.int32).astype(jnp.int16)


def bucket(blocks, rows, dest_ref, counts, members):
    stride = rows + UNROLL

    def clear(b, carry):
        counts[b] = 0
        return carry

    lax.fori_loop(0, blocks, clear, 0)

    def place(r, carry):
        target = dest_ref[r]
        count = counts[target]
        members[target * stride + count] = r
        counts[target] = count + 1
        return carry

    lax.fori_loop(0, rows, place, 0, unroll=16)

    def pad(b, carry):
        end = b * stride + counts[b]
        for extra in range(UNROLL - 1):
            members[end + extra] = rows
        return carry

    lax.fori_loop(0, blocks, pad, 0)


def block_sums(target, at, stride, dens, flow, counts, members):
    first = target * stride

    def body(turn, totals):
        totals = list(totals)
        for u in range(UNROLL):
            row = members[first + turn * UNROLL + u]
            rho = dens[row, at, :].astype(jnp.float32)
            ux = flow[row, 0, at, :].astype(jnp.float32)
            uy = flow[row, 1, at, :].astype(jnp.float32)
            uz = flow[row, 2, at, :].astype(jnp.float32)
            excess = flow[row, 3, at, :].astype(jnp.float32)
            mx, my, mz = rho * ux, rho * uy, rho * uz
            for i, term in enumerate((mx * ux, my * uy, mz * uz, mx * uy, mx * uz, my * uz, excess)):
                totals[i] = totals[i] + term
        return tuple(totals)

    zero = jnp.zeros((TILE, LANES), jnp.float32)
    turns = (counts[target] + (UNROLL - 1)) // UNROLL
    xx, yy, zz, xy, xz, yz, excess = lax.fori_loop(0, turns, body, (zero,) * 7)
    return xx + excess, yy + excess, zz + excess, xy, xz, yz


def leaving_kernel(blocks, halves, dest_ref, density_ref, flow_ref, *refs):
    sends, (dens, flow, counts, members) = refs[:halves], refs[halves:halves + 4]
    dest, staged, sems, dest_sem = refs[halves + 4:]
    rows, steps = density_ref.shape[0], density_ref.shape[1]
    per_half = steps // TILE // halves
    span = steps // halves
    fetch = pltpu.make_async_copy(dest_ref, dest, dest_sem)
    fetch.start()
    copies = []
    for k in range(steps // TILE):
        at = pl.ds(k * TILE, TILE)
        pair = (
            pltpu.make_async_copy(density_ref.at[:, at, :], dens.at[pl.ds(0, rows), at, :], sems.at[k, 0]),
            pltpu.make_async_copy(flow_ref.at[:, :, at, :], flow.at[pl.ds(0, rows), :, at, :], sems.at[k, 1]),
        )
        for copy in pair:
            copy.start()
        copies.append(pair)

    dens[rows] = jnp.zeros_like(dens[rows])
    flow[rows] = jnp.zeros_like(flow[rows])
    fetch.wait()
    bucket(blocks, rows, dest, counts, members)
    for half in range(halves):
        largest = jnp.zeros((TILE, LANES), jnp.float32)
        for k in range(per_half):
            tile = half * per_half + k
            for copy in copies[tile]:
                copy.wait()

            def block(i, top):
                pieces = slot_sums(half, i, 1, tile, dens, flow, counts, members)
                for c, piece in enumerate(pieces):
                    staged[rows_at((i * COMPS + c) * span + k * TILE), :] = piece
                    top = jnp.maximum(top, jnp.abs(piece))
                return top

            largest = lax.fori_loop(0, blocks // 2, block, largest)
        write_codes(largest, staged, sends[half], blocks // 2 * COMPS * span)


def staying_kernel(blocks, halves, dens, flow, counts, members, *outs):
    steps = dens.shape[1]
    per_half = steps // TILE // halves
    span = steps // halves
    for half in range(halves):
        for k in range(per_half):
            def block(i, carry):
                pieces = slot_sums(half, i, 0, half * per_half + k, dens, flow, counts, members)
                for c, piece in enumerate(pieces):
                    outs[half][rows_at((i * COMPS + c) * span + k * TILE), :] = piece
                return carry

            lax.fori_loop(0, blocks // 2, block, 0)


def slot_sums(half, slot, leaving, tile, dens, flow, counts, members):
    bit = half
    target = lax.axis_index("blk") ^ with_bit(slot, bit, leaving)
    at = slice(tile * TILE, (tile + 1) * TILE)
    return block_sums(target, at, dens.shape[0] - 1 + UNROLL, dens, flow, counts, members)


def leaving_sums(density, flow_rest, targets, blocks, halves):
    rows, steps, _ = density.shape
    size = blocks // 2 * COMPS * (steps // halves)
    made = pl.pallas_call(
        functools.partial(leaving_kernel, blocks, halves),
        out_shape=[pltpu.VMEM((size + TILE, LANES), jnp.int16)] * halves + [
            pltpu.VMEM((rows + 1, steps, LANES), density.dtype),
            pltpu.VMEM((rows + 1, flow_rest.shape[1], steps, LANES), flow_rest.dtype),
            pltpu.SMEM((blocks,), jnp.int32),
            pltpu.SMEM((blocks * (rows + UNROLL),), jnp.int32),
        ],
        in_specs=[pl.BlockSpec(memory_space=pltpu.HBM)] * 3,
        out_specs=[whole()] * (halves + 2) + [scalars()] * 2,
        scratch_shapes=[
            pltpu.SMEM((rows,), jnp.int32),
            pltpu.VMEM((size, LANES), jnp.float32),
            pltpu.SemaphoreType.DMA((steps // TILE, 2)),
            pltpu.SemaphoreType.DMA(()),
        ],
        compiler_params=params(24),
        name="leaving_sums",
    )(pltpu.with_memory_space_constraint(targets, pltpu.HBM), pltpu.with_memory_space_constraint(density, pltpu.HBM), pltpu.with_memory_space_constraint(flow_rest, pltpu.HBM))
    return list(made[:halves]), list(made[halves:])


def staying_sums(held, blocks, halves):
    size = blocks // 2 * COMPS * (held[0].shape[1] // halves)
    return pl.pallas_call(
        functools.partial(staying_kernel, blocks, halves),
        out_shape=[jax.ShapeDtypeStruct((size, LANES), jnp.float32)] * halves,
        in_specs=[whole()] * 2 + [scalars()] * 2,
        out_specs=[whole()] * halves,
        compiler_params=params(16),
        name="staying_sums",
    )(*held)


def total_at(got, kept, factor, where):
    return kept[rows_at(where), :] + decode(got[rows_at(where), :], factor)


def send_kernel(count, position, size, got, kept, send, staged):
    factor = decode_factor(got[count * size:count * size + TILE, :])

    def block(i, top):
        def tile(k, top):
            piece = total_at(got, kept, factor, with_bit(i, position, 1) * size + k * TILE)
            staged[rows_at(i * size + k * TILE), :] = piece
            return jnp.maximum(top, jnp.abs(piece))

        return lax.fori_loop(0, size // TILE, tile, top, unroll=4)

    largest = lax.fori_loop(0, count // 2, block, jnp.zeros((TILE, LANES), jnp.float32))
    write_codes(largest, staged, send, count // 2 * size)


def keep_kernel(count, position, size, got, kept, keep):
    factor = decode_factor(got[count * size:count * size + TILE, :])

    def block(i, carry):
        def tile(k, carry):
            keep[rows_at(i * size + k * TILE), :] = total_at(got, kept, factor, with_bit(i, position, 0) * size + k * TILE)
            return carry

        return lax.fori_loop(0, size // TILE, tile, carry, unroll=4)

    lax.fori_loop(0, count // 2, block, 0)


def merge(got, kept, count, position, size):
    rows = count // 2 * size
    send = pl.pallas_call(
        functools.partial(send_kernel, count, position, size),
        out_shape=jax.ShapeDtypeStruct((rows + TILE, LANES), jnp.int16),
        in_specs=[whole()] * 2,
        out_specs=whole(),
        scratch_shapes=[pltpu.VMEM((rows, LANES), jnp.float32)],
        compiler_params=params(),
        name="merge_sent",
    )(got, kept)
    keep = pl.pallas_call(
        functools.partial(keep_kernel, count, position, size),
        out_shape=jax.ShapeDtypeStruct((rows, LANES), jnp.float32),
        in_specs=[whole()] * 2,
        out_specs=whole(),
        compiler_params=params(),
        name="merge_kept",
    )(got, kept)
    return send, keep


def project(half, got_ref, kept_ref, proj_ref, weights_ref, totals):
    observers = weights_ref.shape[0]
    span = kept_ref.shape[0] // COMPS
    factor = decode_factor(got_ref[COMPS * span:COMPS * span + TILE, :])

    def fill(k, carry):
        where = rows_at(k * TILE)
        totals[where, :] = kept_ref[where, :] + decode(got_ref[where, :], factor)
        return carry

    lax.fori_loop(0, COMPS * span // TILE, fill, 0, unroll=4)
    lane = lax.broadcasted_iota(jnp.int32, (span, LANES), 1) % observers
    ones = jnp.ones((2 * LANES, LANES), jnp.bfloat16)
    at = slice(half * span, (half + 1) * span)
    parts = [totals[c * span:(c + 1) * span, :] for c in range(COMPS)]
    value = jnp.zeros((span, LANES), jnp.float32)
    for group in range(0, observers, GROUP):
        rows = []
        for o in range(group, group + GROUP):
            moment = proj_ref[o:o + 1, :] * parts[0]
            for c in range(1, COMPS):
                moment = moment + proj_ref[c * observers + o:c * observers + o + 1, :] * parts[c]
            term = weights_ref[o, at, :].astype(jnp.float32) * moment
            high = term.astype(jnp.bfloat16)
            low = (term - high.astype(jnp.float32)).astype(jnp.bfloat16)
            rows.append(jnp.concatenate([high, low], axis=1))
        sums = jnp.dot(jnp.concatenate(rows, axis=0), ones, preferred_element_type=jnp.float32)
        for u in range(GROUP):
            value = jnp.where(lane == group + u, sums[u * span:(u + 1) * span], value)
    return value


def first_kernel(proj_ref, got_ref, kept_ref, weights_ref, out_ref, totals):
    out_ref[...] = project(0, got_ref, kept_ref, proj_ref, weights_ref, totals)


def last_kernel(slabs, per_device, proj_ref, got_ref, kept_ref, weights_ref, first_ref, bins_ref, out_ref, totals):
    observers, steps, _ = weights_ref.shape
    source = jnp.concatenate(
        [first_ref[...], project(1, got_ref, kept_ref, proj_ref, weights_ref, totals)], axis=0
    )
    lead, period = 8, slabs * steps
    blank = jnp.zeros((lead, LANES), jnp.float32)
    value = jnp.concatenate([blank, source, blank], axis=0)
    size = value.shape[0]
    value = pltpu.roll(value, size - 1, 0) - 2.0 * value + pltpu.roll(value, 1, 0)
    value = jnp.concatenate([value, blank], axis=0)
    delay = bins_ref[...] + (lax.axis_index("tm") * steps + period - lead)
    delay = jnp.broadcast_to(jnp.where(delay >= period, delay - period, delay), (lead, LANES))
    delay = jnp.where(delay >= period, delay - period, delay)
    shift = 1
    while shift < lead:
        late = jnp.concatenate([(delay & shift) != 0] * (value.shape[0] // lead), axis=0)
        value = jnp.where(late, pltpu.roll(value, shift, 0), value)
        shift *= 2
    tiles = [value[k:k + lead] for k in range(0, value.shape[0], lead)]
    while shift < period // 2:
        far, late = shift // lead, (delay & shift) != 0
        padded = [blank] * far + tiles + [blank] * far
        tiles = [jnp.where(late, padded[k], padded[k + far]) for k in range(len(tiles) + far)]
        shift *= 2
    half = shift // lead
    tiles = tiles + [blank] * (2 * half - len(tiles))
    upper = lax.broadcasted_iota(jnp.int32, (lead, LANES), 1) >= observers
    late = ((delay & shift) != 0) != upper
    tiles = [jnp.where(late, tiles[k + half], tiles[k]) for k in range(half)]
    across = jnp.concatenate(tiles, axis=0).T
    rows = out_ref.shape[1]
    lane = lax.broadcasted_iota(jnp.int32, (per_device, LANES), 1)
    low = lane < steps
    blocks = observers // per_device
    for b in range(blocks):
        for pair in range(period // LANES):
            first = pair * observers + b * per_device
            mine = across[first:first + per_device]
            turned = pltpu.roll(mine, steps, 1)
            if rows < per_device:
                down = jnp.concatenate([mine[rows:], mine[:rows]], axis=0)
                down_turned = jnp.concatenate([turned[rows:], turned[:rows]], axis=0)
                out_ref[2 * pair * blocks + b] = jnp.where(low, mine, down_turned)[:rows]
                out_ref[(2 * pair + 1) * blocks + b] = jnp.where(low, turned, down)[:rows]
            else:
                out_ref[2 * pair * blocks + b] = mine
                out_ref[(2 * pair + 1) * blocks + b] = turned


def sources(projector, got, kept, weights, bins, blocks, slabs):
    observers = weights.shape[0]
    per_device = observers // blocks
    rows = per_device // 2 if per_device % 2 == 0 else per_device
    size = kept[0].shape[0]
    first = pl.pallas_call(
        first_kernel,
        out_shape=jax.ShapeDtypeStruct((size // COMPS, LANES), jnp.float32),
        in_specs=[whole()] * 4,
        out_specs=whole(),
        scratch_shapes=[pltpu.VMEM((size, LANES), jnp.float32)],
        compiler_params=params(),
        name="first_sources",
    )(projector, got[0], kept[0], weights)
    return pl.pallas_call(
        functools.partial(last_kernel, slabs, per_device),
        out_shape=jax.ShapeDtypeStruct((blocks * slabs, rows, LANES), jnp.float32),
        in_specs=[whole()] * 6,
        out_specs=whole(),
        scratch_shapes=[pltpu.VMEM((size, LANES), jnp.float32)],
        compiler_params=params(),
        name="last_sources",
    )(projector, got[1], kept[1], weights, first, bins)


def record_kernel(got_ref, out_ref):
    per_device, steps = out_ref.shape
    total = got_ref[0]
    for k in range(1, got_ref.shape[0]):
        total = total + got_ref[k]
    rows = total.shape[0]
    out_ref[:rows, :] = total[:, :steps]
    if rows < per_device:
        out_ref[rows:, :] = total[:, steps:]


def records(got, per_device, steps):
    return pl.pallas_call(
        record_kernel,
        out_shape=jax.ShapeDtypeStruct((per_device, steps), jnp.float32),
        in_specs=[whole()],
        out_specs=whole(),
        compiler_params=params(),
        name="records",
    )(got)


def body(density, flow_rest, dest, weights, directions, bins):
    blocks, slabs = lax.axis_size("blk"), lax.axis_size("tm")
    steps = density.shape[1]
    observers = bins.shape[0]

    def swap(values, bit):
        return lax.ppermute(values, "blk", [(i, i ^ (1 << bit)) for i in range(blocks)])

    stages = blocks.bit_length() - 1
    orders = [list(range(stages)) for _ in range(2)]
    orders[1][:2] = [1, 0]
    size = COMPS * (steps // 2)
    bits = tuple(order[0] for order in orders)
    sends, held = leaving_sums(density, flow_rest, dest[:, 0], blocks, 2)
    kept = staying_sums(held, blocks, 2)
    got = [swap(send, order[0]) for send, order in zip(sends, orders)]
    count = blocks // 2
    for stage in range(1, stages):
        places = [sorted(order[stage:]).index(order[stage]) for order in orders]
        made = [merge(got[p], kept[p], count, places[p], size) for p in range(2)]
        got = [swap(made[p][0], orders[p][stage]) for p in range(2)]
        kept = [made[p][1] for p in range(2)]
        count //= 2

    d1, d2, d3 = [jnp.broadcast_to(directions[:, c:c + 1], (observers, LANES)) for c in range(3)]
    projector = jnp.concatenate(
        [d1 * d1, d2 * d2, d3 * d3, 2.0 * d1 * d2, 2.0 * d1 * d3, 2.0 * d2 * d3], axis=0
    )
    chunks = sources(projector, got, kept, weights[0], jnp.concatenate([bins.T] * 2, axis=1), blocks, slabs)
    chunks = lax.all_to_all(chunks, ("tm", "blk"), split_axis=0, concat_axis=0, tiled=True)
    return records(chunks, observers // blocks, steps)


def solution(mesh):
    placed = (
        P("blk", "tm", None),
        P("blk", None, "tm", None),
        P("blk", None),
        P("blk", None, "tm", None),
        P(),
        P(None, "blk"),
    )
    return jax.shard_map(
        body, mesh=mesh, in_specs=placed, out_specs=P("blk", "tm"), check_vma=False
    )
```

```python
import functools

import jax
import jax.numpy as jnp
from jax import lax
from jax.experimental import pallas as pl
from jax.experimental.pallas import tpu as pltpu
from jax.sharding import PartitionSpec as P

COMPS = 6
TILE = 16
LANES = 128
GROUP = 8
UNROLL = 6
GRAIN = 128.0
TOP = 32764.0
FLOOR = 1e-33


def whole():
    return pl.BlockSpec(memory_space=pltpu.VMEM)


def scalars():
    return pl.BlockSpec(memory_space=pltpu.SMEM)


def params(mebibytes=40):
    return pltpu.CompilerParams(vmem_limit_bytes=mebibytes * 1024 * 1024)


def scale_code(largest):
    return jnp.ceil(jnp.log(jnp.maximum(largest, FLOOR)) * GRAIN)


def encode(values, inverse):
    return jnp.round(values * inverse).astype(jnp.int32).astype(jnp.int16)


def encode_factor(code):
    return jnp.exp(code * (-1.0 / GRAIN)) * TOP


def decode_factor(code16):
    code = code16.astype(jnp.int32).astype(jnp.float32)
    return jnp.exp(code * (1.0 / GRAIN)) * (1.0 / TOP)


def decode(code16, factor):
    return code16.astype(jnp.int32).astype(jnp.float32) * factor


def with_bit(index, position, bit):
    low = index & ((1 << position) - 1)
    return ((index >> position) << (position + 1)) | (bit << position) | low


def rows_at(start, size=TILE):
    return pl.ds(pl.multiple_of(start, TILE), size)


def write_codes(largest, staged, send_ref, rows):
    code = scale_code(largest)
    inverse = encode_factor(code)

    def step(k, carry):
        where = rows_at(k * TILE)
        send_ref[where, :] = encode(staged[where, :], inverse)
        return carry

    lax.fori_loop(0, rows // TILE, step, 0, unroll=8)
    send_ref[rows:rows + TILE, :] = code.astype(jnp.int32).astype(jnp.int16)


def bucket(blocks, rows, dest_ref, counts, members):
    stride = rows + UNROLL

    def clear(b, carry):
        counts[b] = 0
        return carry

    lax.fori_loop(0, blocks, clear, 0)

    def place(r, carry):
        target = dest_ref[r]
        count = counts[target]
        members[target * stride + count] = r
        counts[target] = count + 1
        return carry

    lax.fori_loop(0, rows, place, 0, unroll=16)

    def pad(b, carry):
        end = b * stride + counts[b]
        for extra in range(UNROLL - 1):
            members[end + extra] = rows
        return carry

    lax.fori_loop(0, blocks, pad, 0)


def block_sums(target, at, stride, dens, flow, counts, members):
    first = target * stride

    def body(turn, totals):
        totals = list(totals)
        for u in range(UNROLL):
            row = members[first + turn * UNROLL + u]
            rho = dens[row, at, :].astype(jnp.float32)
            ux = flow[row, 0, at, :].astype(jnp.float32)
            uy = flow[row, 1, at, :].astype(jnp.float32)
            uz = flow[row, 2, at, :].astype(jnp.float32)
            excess = flow[row, 3, at, :].astype(jnp.float32)
            mx, my, mz = rho * ux, rho * uy, rho * uz
            for i, term in enumerate((mx * ux, my * uy, mz * uz, mx * uy, mx * uz, my * uz, excess)):
                totals[i] = totals[i] + term
        return tuple(totals)

    zero = jnp.zeros((TILE, LANES), jnp.float32)
    turns = (counts[target] + (UNROLL - 1)) // UNROLL
    xx, yy, zz, xy, xz, yz, excess = lax.fori_loop(0, turns, body, (zero,) * 7)
    return xx + excess, yy + excess, zz + excess, xy, xz, yz


def leaving_kernel(blocks, halves, dest_ref, density_ref, flow_ref, *refs):
    sends, (dens, flow, counts, members) = refs[:halves], refs[halves:halves + 4]
    dest, staged, sems, dest_sem = refs[halves + 4:]
    rows, steps = density_ref.shape[0], density_ref.shape[1]
    per_half = steps // TILE // halves
    span = steps // halves
    fetch = pltpu.make_async_copy(dest_ref, dest, dest_sem)
    fetch.start()
    copies = []
    for k in range(steps // TILE):
        at = pl.ds(k * TILE, TILE)
        pair = (
            pltpu.make_async_copy(density_ref.at[:, at, :], dens.at[pl.ds(0, rows), at, :], sems.at[k, 0]),
            pltpu.make_async_copy(flow_ref.at[:, :, at, :], flow.at[pl.ds(0, rows), :, at, :], sems.at[k, 1]),
        )
        for copy in pair:
            copy.start()
        copies.append(pair)

    dens[rows] = jnp.zeros_like(dens[rows])
    flow[rows] = jnp.zeros_like(flow[rows])
    fetch.wait()
    bucket(blocks, rows, dest, counts, members)
    for half in range(halves):
        largest = jnp.zeros((TILE, LANES), jnp.float32)
        for k in range(per_half):
            tile = half * per_half + k
            for copy in copies[tile]:
                copy.wait()

            def block(i, top):
                pieces = slot_sums(half, i, 1, tile, dens, flow, counts, members)
                for c, piece in enumerate(pieces):
                    staged[rows_at((i * COMPS + c) * span + k * TILE), :] = piece
                    top = jnp.maximum(top, jnp.abs(piece))
                return top

            largest = lax.fori_loop(0, blocks // 2, block, largest)
        write_codes(largest, staged, sends[half], blocks // 2 * COMPS * span)


def staying_kernel(blocks, halves, dens, flow, counts, members, *outs):
    steps = dens.shape[1]
    per_half = steps // TILE // halves
    span = steps // halves
    for half in range(halves):
        for k in range(per_half):
            def block(i, carry):
                pieces = slot_sums(half, i, 0, half * per_half + k, dens, flow, counts, members)
                for c, piece in enumerate(pieces):
                    outs[half][rows_at((i * COMPS + c) * span + k * TILE), :] = piece
                return carry

            lax.fori_loop(0, blocks // 2, block, 0)


def slot_sums(half, slot, leaving, tile, dens, flow, counts, members):
    bit = half
    target = lax.axis_index("blk") ^ with_bit(slot, bit, leaving)
    at = slice(tile * TILE, (tile + 1) * TILE)
    return block_sums(target, at, dens.shape[0] - 1 + UNROLL, dens, flow, counts, members)


def leaving_sums(density, flow_rest, targets, blocks, halves):
    rows, steps, _ = density.shape
    size = blocks // 2 * COMPS * (steps // halves)
    made = pl.pallas_call(
        functools.partial(leaving_kernel, blocks, halves),
        out_shape=[pltpu.VMEM((size + TILE, LANES), jnp.int16)] * halves + [
            pltpu.VMEM((rows + 1, steps, LANES), density.dtype),
            pltpu.VMEM((rows + 1, flow_rest.shape[1], steps, LANES), flow_rest.dtype),
            pltpu.SMEM((blocks,), jnp.int32),
            pltpu.SMEM((blocks * (rows + UNROLL),), jnp.int32),
        ],
        in_specs=[pl.BlockSpec(memory_space=pltpu.HBM)] * 3,
        out_specs=[whole()] * (halves + 2) + [scalars()] * 2,
        scratch_shapes=[
            pltpu.SMEM((rows,), jnp.int32),
            pltpu.VMEM((size, LANES), jnp.float32),
            pltpu.SemaphoreType.DMA((steps // TILE, 2)),
            pltpu.SemaphoreType.DMA(()),
        ],
        compiler_params=params(24),
        name="leaving_sums",
    )(pltpu.with_memory_space_constraint(targets, pltpu.HBM), pltpu.with_memory_space_constraint(density, pltpu.HBM), pltpu.with_memory_space_constraint(flow_rest, pltpu.HBM))
    return list(made[:halves]), list(made[halves:])


def staying_sums(held, blocks, halves):
    size = blocks // 2 * COMPS * (held[0].shape[1] // halves)
    return pl.pallas_call(
        functools.partial(staying_kernel, blocks, halves),
        out_shape=[jax.ShapeDtypeStruct((size, LANES), jnp.float32)] * halves,
        in_specs=[whole()] * 2 + [scalars()] * 2,
        out_specs=[whole()] * halves,
        compiler_params=params(16),
        name="staying_sums",
    )(*held)


def total_at(got, kept, factor, where):
    return kept[rows_at(where), :] + decode(got[rows_at(where), :], factor)


def send_kernel(count, position, size, got, kept, send, staged):
    factor = decode_factor(got[count * size:count * size + TILE, :])

    def block(i, top):
        def tile(k, top):
            piece = total_at(got, kept, factor, with_bit(i, position, 1) * size + k * TILE)
            staged[rows_at(i * size + k * TILE), :] = piece
            return jnp.maximum(top, jnp.abs(piece))

        return lax.fori_loop(0, size // TILE, tile, top, unroll=4)

    largest = lax.fori_loop(0, count // 2, block, jnp.zeros((TILE, LANES), jnp.float32))
    write_codes(largest, staged, send, count // 2 * size)


def keep_kernel(count, position, size, got, kept, keep):
    factor = decode_factor(got[count * size:count * size + TILE, :])

    def block(i, carry):
        def tile(k, carry):
            keep[rows_at(i * size + k * TILE), :] = total_at(got, kept, factor, with_bit(i, position, 0) * size + k * TILE)
            return carry

        return lax.fori_loop(0, size // TILE, tile, carry, unroll=4)

    lax.fori_loop(0, count // 2, block, 0)


def merge(got, kept, count, position, size):
    rows = count // 2 * size
    send = pl.pallas_call(
        functools.partial(send_kernel, count, position, size),
        out_shape=jax.ShapeDtypeStruct((rows + TILE, LANES), jnp.int16),
        in_specs=[whole()] * 2,
        out_specs=whole(),
        scratch_shapes=[pltpu.VMEM((rows, LANES), jnp.float32)],
        compiler_params=params(),
        name="merge_sent",
    )(got, kept)
    keep = pl.pallas_call(
        functools.partial(keep_kernel, count, position, size),
        out_shape=jax.ShapeDtypeStruct((rows, LANES), jnp.float32),
        in_specs=[whole()] * 2,
        out_specs=whole(),
        compiler_params=params(),
        name="merge_kept",
    )(got, kept)
    return send, keep


def project(half, got_ref, kept_ref, proj_ref, weights_ref, totals):
    observers = weights_ref.shape[0]
    span = kept_ref.shape[0] // COMPS
    factor = decode_factor(got_ref[COMPS * span:COMPS * span + TILE, :])

    def fill(k, carry):
        where = rows_at(k * TILE)
        totals[where, :] = kept_ref[where, :] + decode(got_ref[where, :], factor)
        return carry

    lax.fori_loop(0, COMPS * span // TILE, fill, 0, unroll=4)
    lane = lax.broadcasted_iota(jnp.int32, (span, LANES), 1) % observers
    ones = jnp.ones((2 * LANES, LANES), jnp.bfloat16)
    at = slice(half * span, (half + 1) * span)
    parts = [totals[c * span:(c + 1) * span, :] for c in range(COMPS)]
    value = jnp.zeros((span, LANES), jnp.float32)
    for group in range(0, observers, GROUP):
        rows = []
        for o in range(group, group + GROUP):
            moment = proj_ref[o:o + 1, :] * parts[0]
            for c in range(1, COMPS):
                moment = moment + proj_ref[c * observers + o:c * observers + o + 1, :] * parts[c]
            term = weights_ref[o, at, :].astype(jnp.float32) * moment
            high = term.astype(jnp.bfloat16)
            low = (term - high.astype(jnp.float32)).astype(jnp.bfloat16)
            rows.append(jnp.concatenate([high, low], axis=1))
        sums = jnp.dot(jnp.concatenate(rows, axis=0), ones, preferred_element_type=jnp.float32)
        for u in range(GROUP):
            value = jnp.where(lane == group + u, sums[u * span:(u + 1) * span], value)
    return value


def first_kernel(proj_ref, got_ref, kept_ref, weights_ref, out_ref, totals):
    out_ref[...] = project(0, got_ref, kept_ref, proj_ref, weights_ref, totals)


def last_kernel(slabs, per_device, proj_ref, got_ref, kept_ref, weights_ref, first_ref, bins_ref, out_ref, totals):
    observers, steps, _ = weights_ref.shape
    source = jnp.concatenate(
        [first_ref[...], project(1, got_ref, kept_ref, proj_ref, weights_ref, totals)], axis=0
    )
    lead, period = 8, slabs * steps
    blank = jnp.zeros((lead, LANES), jnp.float32)
    value = jnp.concatenate([blank, source, blank], axis=0)
    size = value.shape[0]
    value = pltpu.roll(value, size - 1, 0) - 2.0 * value + pltpu.roll(value, 1, 0)
    value = jnp.concatenate([value, blank], axis=0)
    delay = bins_ref[...] + (lax.axis_index("tm") * steps + period - lead)
    delay = jnp.broadcast_to(jnp.where(delay >= period, delay - period, delay), (lead, LANES))
    delay = jnp.where(delay >= period, delay - period, delay)
    shift = 1
    while shift < lead:
        late = jnp.concatenate([(delay & shift) != 0] * (value.shape[0] // lead), axis=0)
        value = jnp.where(late, pltpu.roll(value, shift, 0), value)
        shift *= 2
    tiles = [value[k:k + lead] for k in range(0, value.shape[0], lead)]
    while shift < period // 2:
        far, late = shift // lead, (delay & shift) != 0
        padded = [blank] * far + tiles + [blank] * far
        tiles = [jnp.where(late, padded[k], padded[k + far]) for k in range(len(tiles) + far)]
        shift *= 2
    half = shift // lead
    tiles = tiles + [blank] * (2 * half - len(tiles))
    upper = lax.broadcasted_iota(jnp.int32, (lead, LANES), 1) >= observers
    late = ((delay & shift) != 0) != upper
    tiles = [jnp.where(late, tiles[k + half], tiles[k]) for k in range(half)]
    across = jnp.concatenate(tiles, axis=0).T
    rows = out_ref.shape[1]
    lane = lax.broadcasted_iota(jnp.int32, (per_device, LANES), 1)
    low = lane < steps
    blocks = observers // per_device
    for b in range(blocks):
        for pair in range(period // LANES):
            first = pair * observers + b * per_device
            mine = across[first:first + per_device]
            turned = pltpu.roll(mine, steps, 1)
            if rows < per_device:
                down = jnp.concatenate([mine[rows:], mine[:rows]], axis=0)
                down_turned = jnp.concatenate([turned[rows:], turned[:rows]], axis=0)
                out_ref[2 * pair * blocks + b] = jnp.where(low, mine, down_turned)[:rows]
                out_ref[(2 * pair + 1) * blocks + b] = jnp.where(low, turned, down)[:rows]
            else:
                out_ref[2 * pair * blocks + b] = mine
                out_ref[(2 * pair + 1) * blocks + b] = turned


def sources(projector, got, kept, weights, bins, blocks, slabs):
    observers = weights.shape[0]
    per_device = observers // blocks
    rows = per_device // 2 if per_device % 2 == 0 else per_device
    size = kept[0].shape[0]
    first = pl.pallas_call(
        first_kernel,
        out_shape=jax.ShapeDtypeStruct((size // COMPS, LANES), jnp.float32),
        in_specs=[whole()] * 4,
        out_specs=whole(),
        scratch_shapes=[pltpu.VMEM((size, LANES), jnp.float32)],
        compiler_params=params(),
        name="first_sources",
    )(projector, got[0], kept[0], weights)
    return pl.pallas_call(
        functools.partial(last_kernel, slabs, per_device),
        out_shape=jax.ShapeDtypeStruct((blocks * slabs, rows, LANES), jnp.float32),
        in_specs=[whole()] * 6,
        out_specs=whole(),
        scratch_shapes=[pltpu.VMEM((size, LANES), jnp.float32)],
        compiler_params=params(),
        name="last_sources",
    )(projector, got[1], kept[1], weights, first, bins)


def record_kernel(got_ref, out_ref):
    per_device, steps = out_ref.shape
    total = got_ref[0]
    for k in range(1, got_ref.shape[0]):
        total = total + got_ref[k]
    rows = total.shape[0]
    out_ref[:rows, :] = total[:, :steps]
    if rows < per_device:
        out_ref[rows:, :] = total[:, steps:]


def records(got, per_device, steps):
    return pl.pallas_call(
        record_kernel,
        out_shape=jax.ShapeDtypeStruct((per_device, steps), jnp.float32),
        in_specs=[whole()],
        out_specs=whole(),
        compiler_params=params(),
        name="records",
    )(got)


def body(density, flow_rest, dest, weights, directions, bins):
    blocks, slabs = lax.axis_size("blk"), lax.axis_size("tm")
    steps = density.shape[1]
    observers = bins.shape[0]

    def swap(values, bit):
        return lax.ppermute(values, "blk", [(i, i ^ (1 << bit)) for i in range(blocks)])

    stages = blocks.bit_length() - 1
    orders = [list(range(stages)) for _ in range(2)]
    orders[1][:2] = [1, 0]
    size = COMPS * (steps // 2)
    bits = tuple(order[0] for order in orders)
    sends, held = leaving_sums(density, flow_rest, dest[:, 0], blocks, 2)
    kept = staying_sums(held, blocks, 2)
    got = [swap(send, order[0]) for send, order in zip(sends, orders)]
    count = blocks // 2
    for stage in range(1, stages):
        places = [sorted(order[stage:]).index(order[stage]) for order in orders]
        made = [merge(got[p], kept[p], count, places[p], size) for p in range(2)]
        got = [swap(made[p][0], orders[p][stage]) for p in range(2)]
        kept = [made[p][1] for p in range(2)]
        count //= 2

    d1, d2, d3 = [jnp.broadcast_to(directions[:, c:c + 1], (observers, LANES)) for c in range(3)]
    projector = jnp.concatenate(
        [d1 * d1, d2 * d2, d3 * d3, 2.0 * d1 * d2, 2.0 * d1 * d3, 2.0 * d2 * d3], axis=0
    )
    chunks = sources(projector, got, kept, weights[0], jnp.concatenate([bins.T] * 2, axis=1), blocks, slabs)
    chunks = lax.all_to_all(chunks, ("tm", "blk"), split_axis=0, concat_axis=0, tiled=True)
    return records(chunks, observers // blocks, steps)


def solution(mesh):
    placed = (
        P("blk", "tm", None),
        P("blk", None, "tm", None),
        P("blk", None),
        P("blk", None, "tm", None),
        P(),
        P(None, "blk"),
    )
    return jax.shard_map(
        body, mesh=mesh, in_specs=placed, out_specs=P("blk", "tm"), check_vma=False
    )
```
